256 devices in a mesh: dp: 8 (over y, core), tm: 32 (over z, x).
Axes of the slice: x: 4, y: 4, z: 8, core: 2. Of those that a mesh axis runs over, the one named last changes fastest.
Arguments:
- grad_attn: bfloat16 [8, 8192, 1024], P('dp', 'tm'), may hold values from -6 to 6
- route: int32 [8, 8192], P('dp', 'tm'), may hold values from 0 to 8191, as said below
- lengths: int32 [8, 4], P('dp'), may hold values from 1 to 4096, 8192 in all within a row
- conv_pre: bfloat16 [8, 8192, 512], P('dp', 'tm'), may hold values from -6 to 6
- conv_in: bfloat16 [8, 16384, 512], P('dp', 'tm'), may hold values from -6 to 6
- conv_w: bfloat16 [3, 512, 512], replicated, may hold values from -0.15625 to 0.15625
- proj_w: bfloat16 [512, 1024], replicated, may hold values from -0.25 to 0.25
- in_w: bfloat16 [1024, 2048], replicated, may hold values from -0.1875 to 0.1875
- depth_w: bfloat16 [31, 1024], replicated, may hold values from -1 to 1
- depth_gain: bfloat16 [1024], replicated, may hold values from 0.099609375 to 1.8984375
- out_w: bfloat16 [1024, 1024], replicated, may hold values from -0.1875 to 0.1875
Outputs:
- input_grad: float32 [8, 16384, 512], P('dp', 'tm')
- conv_grad: float32 [3, 512, 512], P(None, 'tm')
- proj_grad: float32 [512, 1024], P('tm')
- in_grad: float32 [1024, 2048], P('tm')
- depth_grad: float32 [31, 1024], P(None, 'tm')
- gain_grad: float32 [1024], P('tm')
- out_grad: float32 [1024, 1024], P('tm')
The draws below stay inside these ranges and needn't reach their ends.
Inputs may be any that keep to these rules, and one draw needn't show every extreme that they name: `route`: each row is a permutation of the frames. Of the 256 attention positions on one device, at most 16 hold frames of any one block of 256 consecutive frames, and every block takes at most 16 from one device's positions; in every packed batch this bound is reached. `lengths`: each row sums to 8192.
All inputs are finite; a program needn't handle non-finite values.
Results may differ from the reference program's by a relative error of at most 0.009.
Values may be sent and summed in bfloat16 or wider, within the bound.
A program may use at most 128 MiB of HBM per device.

```python
import math
import jax
import jax.numpy as jnp
import numpy as np
from jax import lax

D = 1024
CF = 512
KW = 31
UTTS = 4
F_DEV = 256
BATCHES = 8
FRAMES = 8192
N_TM = 32


def route_row(row_key):
    owners = N_TM
    per_owner = F_DEV
    mean_load = per_owner // owners
    first_key, second_key, third_key = jax.random.split(row_key, 3)
    quarter = owners // 4
    places = jnp.arange(owners)
    base = jnp.where(places < quarter, 2 * mean_load, jnp.where(places < 3 * quarter, mean_load, 0)).astype(jnp.int32)
    shuffled = jax.random.permutation(first_key, owners)
    counts = jnp.zeros((owners,), jnp.int32).at[shuffled].set(base)
    bounds = jnp.cumsum(counts)
    sorted_offsets = jnp.sum((jnp.arange(per_owner)[:, None] >= bounds[None, :]).astype(jnp.int32), axis=1)
    orders = jax.vmap(lambda owner: jax.random.permutation(jax.random.fold_in(second_key, owner), per_owner))(jnp.arange(owners))
    offsets = sorted_offsets[orders]
    sources = (jnp.arange(owners)[:, None] + offsets) % owners
    tiebreak = jax.random.permutation(third_key, owners * per_owner)
    ranking = sources.reshape(-1).astype(jnp.int32) * (owners * per_owner) + tiebreak.astype(jnp.int32)
    return jnp.argsort(ranking, stable=True).astype(jnp.int32)


def draw_route(key, part):
    row_keys = jax.vmap(lambda batch: jax.random.fold_in(key, batch))(jnp.arange(BATCHES))
    return jax.vmap(route_row)(row_keys)


def shard_levels(key, shape, cuts, smallest, largest):
    loudness, own = 1.0, jax.random.fold_in(key, 6)
    for axis_at, shards_of in cuts:
        heights = jnp.exp(jax.random.uniform(jax.random.fold_in(own, axis_at), (shards_of,), jnp.float32, smallest / len(cuts), largest / len(cuts)))
        loudness = loudness * jnp.repeat(heights, shape[axis_at] // shards_of).reshape([-1 if axis == axis_at else 1 for axis in range(len(shape))])
    return loudness


def split_up(count, total, bound, slope):
    portions = [(1 << 20) // math.isqrt(rank ** slope) + 1 for rank in range(2, count + 1)]
    surplus, given = total - bound - (count - 1), [1] * (count - 1)
    while surplus > 0:
        candidates = [i for i in range(count - 1) if given[i] < bound]
        pool, remaining = sum([portions[i] for i in candidates]), surplus
        for i in candidates:
            addition = min(bound - given[i], max(1, remaining * portions[i] // pool), surplus)
            given[i] = given[i] + addition
            surplus = surplus - addition
    return np.array([bound] + given)


def ragged(rng, amount, total, bound, lean):
    if amount == 2:
        one = jax.random.randint(rng, (), max(1, total - bound), min(bound, total - 1) + 1)
        return jnp.stack([one, total - one])
    sizes = jnp.asarray(split_up(amount, total, bound, lean), jnp.int32)
    pairs = (amount - 1) // 2
    donor, sink = sizes[1:1 + 2 * pairs:2], sizes[2:2 + 2 * pairs:2]
    room = jnp.minimum(donor - 1, bound - sink)
    shifted = jax.random.randint(jax.random.fold_in(rng, 1), (pairs,), 0, 1 << 20) % (room + 1)
    sizes = sizes.at[1:1 + 2 * pairs:2].set(donor - shifted).at[2:2 + 2 * pairs:2].set(sink + shifted)
    return sizes[jax.random.permutation(jax.random.fold_in(rng, 2), amount)]


def centred(rng, shape, scale, limit, cuts=(), kind=jnp.bfloat16):
    values = jax.random.normal(rng, shape, jnp.float32) * scale
    if len(cuts) > 0:
        values = shard_levels(rng, shape, cuts, -0.22, 0.18) * values
    return jnp.clip(values, min=-limit, max=limit).astype(kind)


def setup_inputs(seed: int = 0) -> dict:
    streams_of = jax.random.split(jax.random.key(seed), 12)
    grad_attn = centred(streams_of[0], (BATCHES, FRAMES, D), 1.0, 6.0, ((0, 8), (1, 32)))
    route = draw_route(jax.random.fold_in(streams_of[11], 71), 0)
    lengths = jax.vmap(lambda own: ragged(own, UTTS, FRAMES, FRAMES // 2, 2))(jax.random.split(streams_of[2], BATCHES)).reshape((BATCHES, UTTS)).astype(jnp.int32)
    conv_pre = centred(streams_of[3], (BATCHES, FRAMES, CF), 1.0, 6.0, ((0, 8), (1, 32)))
    conv_in = centred(streams_of[4], (BATCHES, 2 * FRAMES, CF), 1.0, 6.0, ((0, 8), (1, 32)))
    conv_w = centred(streams_of[5], (3, CF, CF), (3 * CF) ** -0.5, 0.15625)
    proj_w = centred(streams_of[6], (CF, D), CF ** -0.5, 0.25)
    in_w = centred(streams_of[7], (D, 2 * D), D ** -0.5, 0.1875)
    depth_w = centred(streams_of[8], (KW, D), KW ** -0.5, 1.0)
    depth_gain = jnp.clip(1.0 + 0.18 * jax.random.normal(streams_of[9], (D,), jnp.float32), 0.099609375, 1.8984375).astype(jnp.bfloat16)
    out_w = centred(streams_of[10], (D, D), D ** -0.5, 0.1875)
    return {"grad_attn": grad_attn, "route": route, "lengths": lengths, "conv_pre": conv_pre, "conv_in": conv_in, "conv_w": conv_w, "proj_w": proj_w, "in_w": in_w, "depth_w": depth_w, "depth_gain": depth_gain, "out_w": out_w}


epsilon = 1e-05

def gelu_exact(value):
    return 0.5 * value * (1.0 + jax.scipy.special.erf(value / math.sqrt(2.0)))

def gelu_slope(value):
    return 0.5 * (1.0 + jax.scipy.special.erf(value / math.sqrt(2.0))) + value * jnp.exp(-0.5 * value * value) / math.sqrt(2.0 * math.pi)

def segment_of(lengths_row, positions):
    bounds = jnp.cumsum(lengths_row).astype(jnp.int32)
    return lax.optimization_barrier(jnp.sum((positions[:, None] >= bounds[None, :]).astype(jnp.int32), axis=1)).astype(jnp.int32)

def backward_batch(rows_grad, order, lengths_row, conv_pre, conv_in, conv_w, proj_w, in_w, depth_w, depth_gain, out_w):
    width = in_w.shape[0]
    frames = order.shape[0]
    kernel = depth_w.shape[0]
    half = (kernel - 1) // 2
    upstream = jnp.zeros((frames, width), jnp.bfloat16).at[order].set(rows_grad)
    positions = jnp.arange(frames, dtype=jnp.int32)
    segment = segment_of(lengths_row, positions)
    edge_fill = jnp.full((half,), -1, jnp.int32)
    padded_seg = jnp.concatenate([edge_fill, segment, edge_fill])
    activ = gelu_exact(conv_pre.astype(jnp.float32)).astype(jnp.bfloat16)
    features = jnp.dot(activ, proj_w, preferred_element_type=jnp.float32).astype(jnp.bfloat16)
    joined = jnp.dot(features, in_w, preferred_element_type=jnp.float32)
    linear = joined[:, :width]
    sigma = jax.nn.sigmoid(joined[:, width:])
    glu_out = (linear * sigma).astype(jnp.bfloat16)
    glu_pad = jnp.pad(glu_out, ((half, half), (0, 0)))
    taps = depth_w.astype(jnp.float32)
    mixed = jnp.zeros((frames, width), jnp.float32)
    for offset in range(kernel):
        linked = (padded_seg[offset:offset + frames] == segment).astype(jnp.float32)[:, None]
        mixed = mixed + taps[offset] * glu_pad[offset:offset + frames].astype(jnp.float32) * linked
    center = lax.optimization_barrier(jnp.mean(mixed, axis=1, keepdims=True))
    spread = lax.optimization_barrier(jnp.mean((mixed - center) ** 2, axis=1, keepdims=True))
    inv_std = 1.0 / jnp.sqrt(spread + epsilon)
    normed = (mixed - center) * inv_std
    gain = depth_gain.astype(jnp.float32)
    scaled = normed * gain
    sig_scaled = jax.nn.sigmoid(scaled)
    swished = (scaled * sig_scaled).astype(jnp.bfloat16)
    out_term = jnp.dot(swished.T, upstream, preferred_element_type=jnp.float32)
    dswish = jnp.dot(upstream, out_w.T, preferred_element_type=jnp.float32)
    dscaled = dswish * sig_scaled * (1.0 + scaled * (1.0 - sig_scaled))
    gain_term = lax.optimization_barrier(jnp.sum(dscaled * normed, axis=0))
    qterm = dscaled * gain
    dmixed_f = inv_std * (qterm - lax.optimization_barrier(jnp.mean(qterm, axis=1, keepdims=True)) - normed * lax.optimization_barrier(jnp.mean(qterm * normed, axis=1, keepdims=True)))
    dmixed_pad = jnp.pad(dmixed_f, ((half, half), (0, 0)))
    dglu = jnp.zeros((frames, width), jnp.float32)
    depth_rows = []
    for offset in range(kernel):
        linked = (padded_seg[offset:offset + frames] == segment).astype(jnp.float32)[:, None]
        depth_rows.append(lax.optimization_barrier(jnp.sum(glu_pad[offset:offset + frames].astype(jnp.float32) * dmixed_f * linked, axis=0)))
        start = 2 * half - offset
        linked_back = (padded_seg[start:start + frames] == segment).astype(jnp.float32)[:, None]
        dglu = dglu + taps[offset] * dmixed_pad[start:start + frames] * linked_back
    depth_term = jnp.stack(depth_rows, axis=0)
    djoined = jnp.concatenate([dglu * sigma, dglu * linear * sigma * (1.0 - sigma)], axis=1).astype(jnp.bfloat16)
    in_term = jnp.dot(features.T, djoined, preferred_element_type=jnp.float32)
    dfeatures = (upstream.astype(jnp.float32) + jnp.dot(djoined, in_w.T, preferred_element_type=jnp.float32)).astype(jnp.bfloat16)
    proj_term = jnp.dot(activ.T, dfeatures, preferred_element_type=jnp.float32)
    dpre = (jnp.dot(dfeatures, proj_w.T, preferred_element_type=jnp.float32) * gelu_slope(conv_pre.astype(jnp.float32))).astype(jnp.bfloat16)
    channels = conv_in.shape[1]
    paired = conv_in.reshape(frames, 2, channels)
    even_rows = paired[:, 0]
    odd_rows = paired[:, 1]
    dpre_next = jnp.concatenate([dpre[1:], jnp.zeros((1, channels), jnp.bfloat16)], axis=0)
    grad_even = jnp.dot(dpre, conv_w[1].T, preferred_element_type=jnp.float32)
    grad_odd = jnp.dot(dpre, conv_w[2].T, preferred_element_type=jnp.float32) + jnp.dot(dpre_next, conv_w[0].T, preferred_element_type=jnp.float32)
    input_rows = jnp.stack([grad_even, grad_odd], axis=1).reshape(2 * frames, channels)
    conv_term = jnp.stack([jnp.dot(odd_rows.T, dpre_next, preferred_element_type=jnp.float32), jnp.dot(even_rows.T, dpre, preferred_element_type=jnp.float32), jnp.dot(odd_rows.T, dpre, preferred_element_type=jnp.float32)], axis=0)
    return ((conv_term, proj_term, in_term, depth_term, gain_term, out_term), input_rows)

def reference(grad_attn, route, lengths, conv_pre, conv_in, conv_w, proj_w, in_w, depth_w, depth_gain, out_w):
    width = in_w.shape[0]
    channels = proj_w.shape[0]
    kernel = depth_w.shape[0]
    start_sums = (jnp.zeros((3, channels, channels), jnp.float32), jnp.zeros((channels, width), jnp.float32), jnp.zeros((width, 2 * width), jnp.float32), jnp.zeros((kernel, width), jnp.float32), jnp.zeros((width,), jnp.float32), jnp.zeros((width, width), jnp.float32))

    def step(carry, inputs):
        terms, input_rows = backward_batch(inputs[0], inputs[1], inputs[2], inputs[3], inputs[4], conv_w, proj_w, in_w, depth_w, depth_gain, out_w)
        return (tuple((total + term for total, term in zip(carry, terms))), input_rows)
    sums, input_grad = lax.scan(step, start_sums, (grad_attn, route, lengths, conv_pre, conv_in))
    factor = 1.0 / math.sqrt(BATCHES * FRAMES)
    return (input_grad, sums[0] * factor, sums[1] * factor, sums[2] * factor, sums[3] * factor, sums[4] * factor, sums[5] * factor)
```

```python
import functools
import math

import jax
import jax.numpy as jnp
from jax import lax
from jax.experimental import pallas as pl
from jax.experimental.pallas import tpu as pltpu
from jax.sharding import PartitionSpec as P

EPS = 1e-05
MESH = pl.DeviceIdType.MESH
BF, F32 = jnp.bfloat16, jnp.float32

F = 256
D = 1024
CF = 512
KW = 31
HALF = 15
H = 16
EXT = F + 2 * H
PAD = EXT + 8
NEXT = F + 8
NEXT16 = F + 16
CAP = 16
NTM, NZ, NX, NY, NC = 32, 8, 4, 4, 2
IDX = 128
PART_ROWS = (32, 64, 48)

NT = (((1,), (1,)), ((), ()))


def dot(a, b):
    return jnp.dot(a, b, preferred_element_type=F32)


def dot_nt(a, b):
    return lax.dot_general(a, b, NT, preferred_element_type=F32)


def block(i, size):
    return pl.ds(pl.multiple_of(i * size, size), size)


def loop(n, body):
    def step(i, carry):
        body(i)
        return carry

    lax.fori_loop(0, n, step, 0)


class Place:
    def __init__(self):
        self.dp = lax.axis_index("dp")
        self.tm = lax.axis_index("tm")
        self.y = lax.div(self.dp, 2)
        self.c = lax.rem(self.dp, 2)
        self.z = lax.div(self.tm, NX)
        self.x = lax.rem(self.tm, NX)

    def at_c(self):
        return (self.y * 2 + (1 - self.c), self.tm)

    def at_y(self, d):
        return (lax.rem(self.y + d, NY) * 2 + self.c, self.tm)

    def at_x(self, d):
        return (self.dp, self.z * NX + lax.rem(self.x + d, NX))

    def at_z(self, d):
        return (self.dp, lax.rem(self.z + d, NZ) * NX + self.x)

    def at_dp(self, d):
        return (lax.rem(self.dp + d, 8), self.tm)

    def at_tm(self, d):
        return (self.dp, lax.rem(self.tm + d, NTM))


def remote(src, dst, send, recv, device):
    return pltpu.make_async_remote_copy(
        src_ref=src, dst_ref=dst, send_sem=send, recv_sem=recv, device_id=device, device_id_type=MESH
    )


def part_scratch(rows):
    tile = (rows, 128)
    return [
        pltpu.VMEM((NC, NY, NZ, NX) + tile, BF),
        pltpu.VMEM((NY, NZ, NX) + tile, BF),
        pltpu.VMEM((3, 4, NX) + tile, BF),
        pltpu.VMEM((3, NY, 4) + tile, BF),
        pltpu.VMEM((4, NX) + tile, BF),
        pltpu.VMEM((NY, 4) + tile, BF),
        pltpu.VMEM((3, 4) + tile, BF),
        pltpu.VMEM((3, 4) + tile, BF),
        pltpu.VMEM((NZ,) + tile, BF),
        pltpu.VMEM((7,) + tile, BF),
        pltpu.VMEM((8,) + tile, BF),
        pltpu.SemaphoreType.DMA((27,)),
        pltpu.SemaphoreType.DMA((27,)),
    ]


class Part:
    def __init__(self, at, refs):
        self.at = at
        (self.g, self.r0, self.r1p, self.r1q, self.a1p, self.a1q, self.r2p, self.r2q) = refs[:8]
        (self.a2, self.r3, self.fin, self.send, self.recv) = refs[8:]
        self.sent = []

    def copy(self, i, src, dst, device):
        return remote(src, dst, self.send.at[i], self.recv.at[i], device)

    def go(self, copies):
        for one in copies:
            one.start()
        self.sent += copies

    def s0(self):
        return [self.copy(0, self.g.at[1 - self.at.c], self.r0, self.at.at_c())]

    def s1(self):
        at, out = self.at, []
        for d in (1, 3, 2):
            y = lax.rem(at.y + d, NY)
            x = lax.rem(at.x + d, NX)
            out.append(
                self.copy(d, self.g.at[at.c, y, pl.ds(0, 4)], self.r1p.at[d - 1], at.at_y(d))
            )
            out.append(
                self.copy(
                    3 + d, self.g.at[at.c, :, pl.ds(4, 4), x], self.r1q.at[d - 1], at.at_x(d)
                )
            )
        return out

    def s2(self):
        at, out = self.at, []
        for d in (1, 3, 2):
            y = lax.rem(at.y + d, NY)
            x = lax.rem(at.x + d, NX)
            out.append(self.copy(6 + d, self.a1p.at[:, x], self.r2p.at[d - 1], at.at_x(d)))
            out.append(self.copy(9 + d, self.a1q.at[y], self.r2q.at[d - 1], at.at_y(d)))
        return out

    def s3(self):
        at, out = self.at, []
        for d in (1, 7, 2, 6, 3, 5, 4):
            z = lax.rem(at.z + d, NZ)
            out.append(self.copy(12 + d, self.a2.at[z], self.r3.at[d - 1], at.at_z(d)))
        return out

    def s4(self):
        at, out = self.at, []
        mine = at.c * NY + at.y
        for d in range(1, 8):
            out.append(self.copy(19 + d, self.fin.at[mine], self.fin.at[mine], at.at_dp(d)))
        return out

    def arrived(self, copies):
        for one in copies:
            one.wait_recv()

    def start(self):
        self.go(self.s0())

    def over_core(self):
        self.arrived(self.s0())
        c = self.at.c

        def add(i):
            y, z = lax.div(i, NZ), lax.rem(i, NZ)
            self.g[c, y, z] = (self.g[c, y, z].astype(F32) + self.r0[y, z].astype(F32)).astype(BF)

        loop(NY * NZ, add)
        self.go(self.s1())

    def over_first(self):
        self.arrived(self.s1())
        c, y, x = self.at.c, self.at.y, self.at.x

        def add(i):
            total = self.g[c, y, i].astype(F32)
            other = self.g[c, i, pl.ds(4, 4), x].astype(F32)
            for d in range(3):
                total = total + self.r1p[d, i].astype(F32)
                other = other + self.r1q[d, i].astype(F32)
            self.a1p[i] = total.astype(BF)
            self.a1q[i] = other.astype(BF)

        loop(4, add)
        self.go(self.s2())

    def over_second(self):
        self.arrived(self.s2())
        y, x = self.at.y, self.at.x

        def add(i):
            total = self.a1p[i, x].astype(F32)
            other = self.a1q[y, i].astype(F32)
            for d in range(3):
                total = total + self.r2p[d, i].astype(F32)
                other = other + self.r2q[d, i].astype(F32)
            self.a2[i] = total.astype(BF)
            self.a2[4 + i] = other.astype(BF)

        loop(4, add)
        self.go(self.s3())

    def over_z(self, factor):
        self.arrived(self.s3())
        total = self.a2[self.at.z].astype(F32)
        for d in range(7):
            total = total + self.r3[d].astype(F32)
        self.fin[self.at.c * NY + self.at.y] = (total * factor).astype(BF)
        self.go(self.s4())

    def gathered(self):
        self.arrived(self.s4())

    def close(self):
        for one in self.sent:
            one.wait_send()


def kernel(
    lengths, route, rows_grad, conv_pre, conv_in, conv_w, proj_w, in_w, depth_w, depth_gain, out_w,
    o_input, o_conv, o_proj, o_in, o_misc, o_out,
    outgoing, incoming, pre, cin_halo, linked, seg, act, slope, feat, linear, sigma, glu, mixed,
    swish_t, dfac, inv, dmix, up, hot, taps, gainsum, dj, df, dpre, feat_t, act_t, sel_t, pairs, dgs,
    a2a_send, a2a_recv, halo_send, halo_recv,
    *parts_refs,
):
    at = Place()
    tm = at.tm
    p_out, p_in, p_rest = (Part(at, parts_refs[13 * i : 13 * i + 13]) for i in range(3))
    left, right = (at.dp, lax.rem(tm + NTM - 1, NTM)), (at.dp, lax.rem(tm + 1, NTM))

    barrier = pltpu.get_barrier_semaphore()

    def greet(d):
        pl.semaphore_signal(barrier, inc=1, device_id=at.at_tm(d + 1), device_id_type=MESH)

    loop(NTM - 1, greet)
    for d in range(1, 8):
        pl.semaphore_signal(barrier, inc=1, device_id=at.at_dp(d), device_id_type=MESH)

    order = route[...]
    owner_row = lax.div(order, F).astype(F32)
    local_row = lax.rem(order, F).astype(F32) + 1.0
    sub = lax.broadcasted_iota(jnp.int32, (F, F), 0)
    lane = lax.broadcasted_iota(jnp.int32, (F, F), 1)
    owners = jnp.broadcast_to(owner_row, (F, F))
    owner_col = jnp.sum(jnp.where(sub == lane, owners, 0.0), axis=1, keepdims=True)
    local_col = jnp.sum(
        jnp.where(sub == lane, jnp.broadcast_to(local_row, (F, F)), 0.0), axis=1, keepdims=True
    )
    before = jnp.where((owners == owner_col) & (sub < lane), 1.0, 0.0)
    slot_row = owner_row * CAP + jnp.sum(before, axis=0, keepdims=True)
    slots = lax.broadcasted_iota(jnp.int32, (NTM * CAP, F), 0).astype(F32)
    hot[...] = jnp.where(slots == slot_row, 1.0, 0.0).astype(BF)

    def pack(j):
        outgoing[:, block(j, 256)] = dot(hot[...], rows_grad[:, block(j, 256)]).astype(BF)

    loop(4, pack)
    outgoing[:, D : D + IDX] = dot(
        hot[...], jnp.broadcast_to(local_col, (F, IDX)).astype(BF)
    ).astype(BF)

    pl.semaphore_wait(barrier, NTM - 1 + 7)

    halos = [
        remote(conv_pre.at[pl.ds(0, H)], pre.at[pl.ds(H + F, H)], halo_send.at[0], halo_recv.at[0], left),
        remote(conv_pre.at[pl.ds(F - H, H)], pre.at[pl.ds(0, H)], halo_send.at[1], halo_recv.at[1], right),
        remote(conv_in.at[pl.ds(2 * F - 16, 16)], cin_halo, halo_send.at[2], halo_recv.at[2], right),
    ]
    for one in halos:
        one.start()

    def routed(d):
        other = lax.rem(tm + d, NTM)
        return remote(
            outgoing.at[block(other, CAP)],
            incoming.at[block(tm, CAP)],
            a2a_send.at[d],
            a2a_recv.at[d],
            (at.dp, other),
        )

    loop(NTM - 1, lambda d: routed(d + 1).start())
    incoming[block(tm, CAP)] = outgoing[block(tm, CAP)]

    bound0 = lengths[0, 0]
    bound1 = bound0 + lengths[0, 1]
    bound2 = bound1 + lengths[0, 2]
    bound3 = bound2 + lengths[0, 3]
    pos = tm * F - H + lax.broadcasted_iota(jnp.int32, (PAD, 128), 0)
    number = sum((pos >= b).astype(jnp.int32) for b in (bound0, bound1, bound2, bound3))
    inside = (pos >= 0) & (pos < F * NTM)
    seg[...] = jnp.where(inside, number, -1)
    for k in range(KW):
        linked[k] = jnp.where(seg[pl.ds(H + k - HALF, NEXT)] == seg[pl.ds(H, NEXT)], 1.0, 0.0)
    taps[pl.ds(0, KW), :] = depth_w[...].astype(F32)
    glu[pl.ds(EXT, 8), :] = jnp.zeros((8, D), F32)
    dmix[pl.ds(EXT, 8), :] = jnp.zeros((8, D), F32)
    dj[pl.ds(F, 16), :] = jnp.zeros((16, 2 * D), BF)

    pre[pl.ds(H, F), :] = conv_pre[...]
    for one in halos[:2]:
        one.wait_recv()

    def gelu(i):
        rows = block(i, 32)
        v = pre[rows, :].astype(F32)
        half = 0.5 * (1.0 + lax.erf(v * (1.0 / math.sqrt(2.0))))
        act[rows, :] = (v * half).astype(BF)
        slope[rows, :] = half + v * jnp.exp(-0.5 * v * v) * (1.0 / math.sqrt(2.0 * math.pi))

    loop(EXT // 32, gelu)

    def features(j):
        feat[:, block(j, 256)] = dot(act[...], proj_w[:, block(j, 256)]).astype(BF)

    loop(4, features)

    def joined(j):
        lin = dot(feat[...], in_w[:, block(j, 256)])
        sig = jax.nn.sigmoid(dot(feat[...], in_w[:, block(4 + j, 256)]))
        linear[:, block(j, 256)] = lin
        sigma[:, block(j, 256)] = sig
        glu[pl.ds(0, EXT), block(j, 256)] = (lin * sig).astype(BF).astype(F32)

    loop(4, joined)

    def mix(j):
        cols = block(j, 128)
        for r in range(0, F, 64):
            total = jnp.zeros((64, 128), F32)
            for k in range(KW):
                total = total + taps[pl.ds(k, 1), cols] * (
                    glu[pl.ds(H + r + k - HALF, 64), cols] * linked[k, pl.ds(r, 64)]
                )
            mixed[pl.ds(r, 64), cols] = total

    loop(8, mix)
    gain = depth_gain[...].astype(F32)

    def norm_all(i):
        rows = block(i, 32)
        v = mixed[rows, :]
        v = v - jnp.mean(v, axis=1, keepdims=True)
        scale = 1.0 / jnp.sqrt(jnp.mean(v * v, axis=1, keepdims=True) + EPS)
        v = v * scale
        inv[rows, :] = jnp.broadcast_to(scale, (32, 128))
        mixed[rows, :] = v
        scaled = v * gain
        s = jax.nn.sigmoid(scaled)
        dfac[rows, :] = s * (1.0 + scaled * (1.0 - s))
        dmix[pl.ds(pl.multiple_of(H + i * 32, 16), 32), :] = scaled * s

    loop(8, norm_all)

    def turn(j):
        cols = block(j, 256)
        swish_t[cols, :] = jnp.transpose(dmix[pl.ds(H, F), cols]).astype(BF)
        feat_t[cols, :] = jnp.transpose(feat[pl.ds(H, F), cols].astype(F32)).astype(BF)

    loop(4, turn)

    def turn_act(j):
        cols = block(j, 256)
        act_t[cols, :] = jnp.transpose(act[pl.ds(H, F), cols].astype(F32)).astype(BF)

    loop(2, turn_act)

    loop(NTM - 1, lambda d: routed(d + 1).wait_recv())
    number = incoming[:, D : D + IDX].astype(F32)
    number = jnp.concatenate([number, number], axis=1)
    wanted = lax.broadcasted_iota(jnp.int32, (NTM * CAP, F), 1).astype(F32) + 1.0
    chosen = jnp.where(number == wanted, 1.0, 0.0)
    sel_t[...] = jnp.transpose(chosen).astype(BF)

    def place(j):
        up[pl.ds(0, F), block(j, 256)] = dot(sel_t[...], incoming[:, block(j, 256)]).astype(BF)

    loop(4, place)
    edge_up = remote(up.at[pl.ds(0, 16)], up.at[pl.ds(F, 16)], halo_send.at[3], halo_recv.at[3], left)
    edge_up.start()

    def dswish(j):
        cols = block(j, 256)
        dfac[:, cols] = dfac[:, cols] * dot_nt(up[pl.ds(0, F), :], out_w[block(j, 256), :])

    loop(4, dswish)
    gainsum[...] = jnp.zeros((8, D), F32)

    def dnorm(i):
        rows = block(i, 32)
        ds = dfac[rows, :]
        v = mixed[rows, :]
        dv = ds * v
        gainsum[...] += dv[0:8] + dv[8:16] + dv[16:24] + dv[24:32]
        q = ds * gain
        q = q - jnp.mean(q, axis=1, keepdims=True) - v * jnp.mean(q * v, axis=1, keepdims=True)
        dmix[pl.ds(pl.multiple_of(H + i * 32, 16), 32), :] = inv[rows, pl.ds(0, 1)] * q

    loop(8, dnorm)
    edges = [
        remote(dmix.at[pl.ds(H, H)], dmix.at[pl.ds(H + F, H)], halo_send.at[4], halo_recv.at[4], left),
        remote(dmix.at[pl.ds(F, H)], dmix.at[pl.ds(0, H)], halo_send.at[5], halo_recv.at[5], right),
    ]
    for one in edges:
        one.start()

    def out_terms(half):
        def body(i):
            b = half * 2 + i
            cols = block(b, 256)
            term = dot(swish_t[...], up[pl.ds(0, F), cols]).astype(BF)
            for s in range(2):
                y = i * 2 + s
                p_out.g[half, y] = term[:, 128 * s : 128 * s + 128].reshape(NZ, NX, 32, 128)

        loop(2, body)

    out_terms(1 - at.c)
    p_out.start()
    out_terms(at.c)

    def depth(j):
        cols = block(j, 128)
        for k in range(KW):
            total = jnp.zeros((8, 128), F32)
            for r in range(0, F, 64):
                term = (
                    glu[pl.ds(H + r + k - HALF, 64), cols]
                    * linked[k, pl.ds(r, 64)]
                    * dmix[pl.ds(H + r, 64), cols]
                )
                total = total + jnp.sum(term.reshape(8, 8, 128), axis=0)
            dgs[k // 8, pl.ds(k % 8, 1), cols] = jnp.sum(total, axis=0, keepdims=True)

    dgs[:, pl.ds(8, 8), :] = jnp.zeros((4, 8, D), F32)
    loop(8, depth)
    dgs[3, pl.ds(7, 1), :] = jnp.sum(gainsum[...], axis=0, keepdims=True)
    p_out.over_core()

    for one in edges:
        one.wait_recv()
    edge_up.wait_recv()

    def dconv(j):
        cols = block(j, 128)
        gates = block(8 + j, 128)
        for r, size in ((0, 64), (64, 64), (128, 64), (192, 64), (256, 8)):
            total = jnp.zeros((size, 128), F32)
            for k in range(KW):
                total = total + taps[pl.ds(KW - 1 - k, 1), cols] * (
                    dmix[pl.ds(H + r + k - HALF, size), cols] * linked[k, pl.ds(r, size)]
                )
            sig = sigma[pl.ds(H + r, size), cols]
            ds = total * sig
            dg = ds * linear[pl.ds(H + r, size), cols] * (1.0 - sig)
            if size == 8:
                zero = jnp.zeros((8, 128), F32)
                ds = jnp.concatenate([ds, zero], axis=0)
                dg = jnp.concatenate([dg, zero], axis=0)
            dj[pl.ds(r, max(size, 16)), cols] = ds.astype(BF)
            dj[pl.ds(r, max(size, 16)), gates] = dg.astype(BF)

    loop(8, dconv)
    p_out.over_first()

    def in_terms(half):
        def body(y):
            term = dot(feat_t[...], dj[pl.ds(0, F), block(half * 4 + y, 256)]).astype(BF)
            for s in range(2):
                p_in.g[half, y, :, :, pl.ds(32 * s, 32), :] = term[
                    :, 128 * s : 128 * s + 128
                ].reshape(NZ, NX, 32, 128)

        loop(4, body)

    in_terms(1 - at.c)
    p_in.start()
    in_terms(at.c)

    def dfeatures(j):
        cols = block(j, 256)
        df[:, cols] = (up[:, cols].astype(F32) + dot_nt(dj[...], in_w[cols, :])).astype(BF)

    loop(4, dfeatures)
    p_in.over_core()

    def dpres(j):
        cols = block(j, 256)
        dpre[:, cols] = (dot_nt(df[...], proj_w[cols, :]) * slope[pl.ds(H, NEXT16), cols]).astype(BF)

    loop(2, dpres)

    halos[2].wait_recv()
    r_f = lax.broadcasted_iota(jnp.int32, (F, 2 * F), 0)
    c_f = lax.broadcasted_iota(jnp.int32, (F, 2 * F), 1)
    r_h = lax.broadcasted_iota(jnp.int32, (F, 16), 0)
    c_h = lax.broadcasted_iota(jnp.int32, (F, 16), 1)
    first = (r_h == 0) & (c_h == 15) & (tm > 0)

    def one_hot(mask):
        return jnp.where(mask, 1.0, 0.0).astype(BF)

    def rest_terms(half):
        def body(i):
            cols = block(half * 2 + i, 256)
            term = dot(act_t[...], df[pl.ds(0, F), cols]).astype(BF)
            for s in range(2):
                y = i * 2 + s
                p_rest.g[half, y, :, :, pl.ds(0, 16), :] = term[
                    :, 128 * s : 128 * s + 128
                ].reshape(NZ, NX, 16, 128)

        loop(2, body)

    def conv_terms(core, row):
        def body(i):
            term = dot(pairs[...], dpre[pl.ds(0, F), block(i, 256)]).astype(BF)
            for s in range(2):
                p_rest.g[core, i * 2 + s, :, :, pl.ds(row, 16), :] = term[
                    :, 128 * s : 128 * s + 128
                ].reshape(NZ, NX, 16, 128)

        loop(2, body)

    rest_terms(0)
    rest_terms(1)
    for tap, core, row in ((0, 0, 16), (1, 0, 32), (2, 1, 16)):
        rows = dot(one_hot(c_f == 2 * r_f + tap - 1), conv_in[...])
        if tap == 0:
            rows = rows + dot(one_hot(first), cin_halo[...])
        pairs[...] = jnp.transpose(rows).astype(BF)
        conv_terms(core, row)
    for z in range(NZ):
        small = dgs[:, :, 128 * z : 128 * z + 128].astype(BF)
        for x in range(NX):
            p_rest.g[1, :, z, x, pl.ds(32, 16), :] = small
    p_rest.start()
    p_out.over_second()
    p_in.over_first()

    r_o = lax.broadcasted_iota(jnp.int32, (2 * F, NEXT16), 0)
    c_o = lax.broadcasted_iota(jnp.int32, (2 * F, NEXT16), 1)
    here = dot(one_hot(r_o == 2 * c_o), dpre[...]).astype(BF)
    here_odd = dot(one_hot(r_o == 2 * c_o + 1), dpre[...]).astype(BF)
    ahead = (r_o == 2 * c_o - 1) & ((c_o < F) | (tm < NTM - 1))
    ahead = dot(one_hot(ahead), dpre[...]).astype(BF)
    o_input[...] = dot_nt(here, conv_w[1])
    o_input[...] += dot_nt(here_odd, conv_w[2])
    o_input[...] += dot_nt(ahead, conv_w[0])

    factor = 1.0 / math.sqrt(F * NTM * 8)
    p_rest.over_core()
    p_out.over_z(factor)
    p_in.over_second()
    p_rest.over_first()
    p_in.over_z(factor)
    p_rest.over_second()
    p_out.gathered()
    for b in range(8):
        o_out[:, 128 * b : 128 * b + 128] = p_out.fin[b].astype(F32)
    p_rest.over_z(factor)
    p_in.gathered()
    for b in range(8):
        for s in range(2):
            o_in[:, 256 * b + 128 * s : 256 * b + 128 * s + 128] = p_in.fin[
                b, pl.ds(32 * s, 32)
            ].astype(F32)
    p_rest.gathered()
    for b in range(8):
        o_proj[:, 128 * b : 128 * b + 128] = p_rest.fin[b, pl.ds(0, 16)].astype(F32)
    for y in range(NY):
        cols = pl.ds(128 * y, 128)
        o_conv[0, :, cols] = p_rest.fin[y, pl.ds(16, 16)].astype(F32)
        o_conv[1, :, cols] = p_rest.fin[y, pl.ds(32, 16)].astype(F32)
        o_conv[2, :, cols] = p_rest.fin[NY + y, pl.ds(16, 16)].astype(F32)
        small = p_rest.fin[NY + y, pl.ds(32, 16)].astype(F32)[0:8]
        mine = jnp.zeros((8, 32), F32)
        for x in range(NX):
            mine = mine + jnp.where(at.x == x, small[:, 32 * x : 32 * x + 32], 0.0)
        o_misc[pl.ds(8 * y, 8), :] = mine

    loop(NTM - 1, lambda d: routed(d + 1).wait_send())
    for one in halos + [edge_up] + edges:
        one.wait_send()
    for part in (p_out, p_in, p_rest):
        part.close()


def per_device(
    grad_attn, route, lengths, conv_pre, conv_in, conv_w, proj_w, in_w, depth_w, depth_gain, out_w
):
    vmem = pl.BlockSpec(memory_space=pltpu.VMEM)
    smem = pl.BlockSpec(memory_space=pltpu.SMEM)
    scratch = [
        pltpu.VMEM((NTM * CAP, D + IDX), BF),
        pltpu.VMEM((NTM * CAP, D + IDX), BF),
        pltpu.VMEM((EXT, CF), BF),
        pltpu.VMEM((16, CF), BF),
        pltpu.VMEM((KW, NEXT, 128), F32),
        pltpu.VMEM((PAD, 128), jnp.int32),
        pltpu.VMEM((EXT, CF), BF),
        pltpu.VMEM((EXT, CF), F32),
        pltpu.VMEM((EXT, D), BF),
        pltpu.VMEM((EXT, D), F32),
        pltpu.VMEM((EXT, D), F32),
        pltpu.VMEM((PAD, D), F32),
        pltpu.VMEM((F, D), F32),
        pltpu.VMEM((D, F), BF),
        pltpu.VMEM((F, D), F32),
        pltpu.VMEM((F, 128), F32),
        pltpu.VMEM((PAD, D), F32),
        pltpu.VMEM((NEXT16, D), BF),
        pltpu.VMEM((NTM * CAP, F), BF),
        pltpu.VMEM((32, D), F32),
        pltpu.VMEM((8, D), F32),
        pltpu.VMEM((NEXT16, 2 * D), BF),
        pltpu.VMEM((NEXT16, D), BF),
        pltpu.VMEM((NEXT16, CF), BF),
        pltpu.VMEM((D, F), BF),
        pltpu.VMEM((CF, F), BF),
        pltpu.VMEM((F, NTM * CAP), BF),
        pltpu.VMEM((CF, F), BF),
        pltpu.VMEM((4, 16, D), F32),
        pltpu.SemaphoreType.DMA((NTM,)),
        pltpu.SemaphoreType.DMA((NTM,)),
        pltpu.SemaphoreType.DMA((6,)),
        pltpu.SemaphoreType.DMA((6,)),
    ]
    for rows in PART_ROWS:
        scratch += part_scratch(rows)
    outs = pl.pallas_call(
        kernel,
        out_shape=[
            jax.ShapeDtypeStruct((2 * F, CF), F32),
            jax.ShapeDtypeStruct((3, 16, CF), F32),
            jax.ShapeDtypeStruct((16, D), F32),
            jax.ShapeDtypeStruct((32, 2 * D), F32),
            jax.ShapeDtypeStruct((32, 32), F32),
            jax.ShapeDtypeStruct((32, D), F32),
        ],
        in_specs=[smem] + [vmem] * 10,
        out_specs=[vmem] * 6,
        scratch_shapes=scratch,
        compiler_params=pltpu.CompilerParams(
            collective_id=0, has_side_effects=True, vmem_limit_bytes=62 * 2**20
        ),
    )(
        lengths, route, grad_attn[0], conv_pre[0], conv_in[0], conv_w, proj_w, in_w, depth_w,
        depth_gain[None], out_w,
    )
    o_input, o_conv, o_proj, o_in, o_misc, o_out = outs
    return (o_input[None], o_conv, o_proj, o_in, o_misc[:KW], o_misc[KW], o_out)


def solution(mesh):
    placed = (
        P("dp", "tm", None),
        P("dp", "tm"),
        P("dp", None),
        P("dp", "tm", None),
        P("dp", "tm", None),
        P(),
        P(),
        P(),
        P(),
        P(),
        P(),
    )
    return jax.shard_map(
        per_device,
        mesh=mesh,
        in_specs=placed,
        out_specs=(
            P("dp", "tm", None),
            P(None, "tm", None),
            P("tm", None),
            P("tm", None),
            P(None, "tm"),
            P("tm"),
            P("tm", None),
        ),
        check_vma=False,
    )
```

```python
import functools
import math

import jax
import jax.numpy as jnp
from jax import lax
from jax.experimental import pallas as pl
from jax.experimental.pallas import tpu as pltpu
from jax.sharding import PartitionSpec as P

EPS = 1e-05
MESH = pl.DeviceIdType.MESH
BF, F32 = jnp.bfloat16, jnp.float32

F = 256
D = 1024
CF = 512
KW = 31
HALF = 15
H = 16
EXT = F + 2 * H
PAD = EXT + 8
NEXT = F + 8
NEXT16 = F + 16
CAP = 16
NTM, NZ, NX, NY, NC = 32, 8, 4, 4, 2
IDX = 128
PART_ROWS = (32, 64, 48)

NT = (((1,), (1,)), ((), ()))


def dot(a, b):
    return jnp.dot(a, b, preferred_element_type=F32)


def dot_nt(a, b):
    return lax.dot_general(a, b, NT, preferred_element_type=F32)


def block(i, size):
    return pl.ds(pl.multiple_of(i * size, size), size)


def loop(n, body):
    def step(i, carry):
        body(i)
        return carry

    lax.fori_loop(0, n, step, 0)


def shift_all(shifts, ref, cols):
    for shift in range(8):
        shifts[shift] = ref[pl.ds(H - HALF + shift, EXT), cols]


def shifted(shifts, tap, start, size):
    return shifts[tap % 8, pl.ds(start + tap - tap % 8, size)]


class Place:
    def __init__(self):
        self.dp = lax.axis_index("dp")
        self.tm = lax.axis_index("tm")
        self.y = lax.div(self.dp, 2)
        self.c = lax.rem(self.dp, 2)
        self.z = lax.div(self.tm, NX)
        self.x = lax.rem(self.tm, NX)

    def at_c(self):
        return (self.y * 2 + (1 - self.c), self.tm)

    def at_y(self, d):
        return (lax.rem(self.y + d, NY) * 2 + self.c, self.tm)

    def at_x(self, d):
        return (self.dp, self.z * NX + lax.rem(self.x + d, NX))

    def at_z(self, d):
        return (self.dp, lax.rem(self.z + d, NZ) * NX + self.x)

    def at_dp(self, d):
        return (lax.rem(self.dp + d, 8), self.tm)

    def at_tm(self, d):
        return (self.dp, lax.rem(self.tm + d, NTM))


def remote(src, dst, send, recv, device):
    return pltpu.make_async_remote_copy(
        src_ref=src, dst_ref=dst, send_sem=send, recv_sem=recv, device_id=device, device_id_type=MESH
    )


def part_scratch(rows):
    tile = (rows, 128)
    return [
        pltpu.VMEM((NC, NY, NZ, NX) + tile, BF),
        pltpu.VMEM((NY, NZ, NX) + tile, BF),
        pltpu.VMEM((3, 2, 2, NX) + tile, BF),
        pltpu.VMEM((3, 2, NY, 2) + tile, BF),
        pltpu.VMEM((4, NX) + tile, BF),
        pltpu.VMEM((NY, 4) + tile, BF),
        pltpu.VMEM((3, 4) + tile, BF),
        pltpu.VMEM((3, 4) + tile, BF),
        pltpu.VMEM((NZ,) + tile, BF),
        pltpu.VMEM((7,) + tile, BF),
        pltpu.VMEM((8,) + tile, BF),
        pltpu.SemaphoreType.DMA((33,)),
        pltpu.SemaphoreType.DMA((33,)),
    ]


class Part:
    def __init__(self, at, refs):
        self.at = at
        (self.g, self.r0, self.r1p, self.r1q, self.a1p, self.a1q, self.r2p, self.r2q) = refs[:8]
        (self.a2, self.r3, self.fin, self.send, self.recv) = refs[8:]
        self.sent = []

    def copy(self, i, src, dst, device):
        return remote(src, dst, self.send.at[i], self.recv.at[i], device)

    def go(self, copies):
        for one in copies:
            one.start()
        self.sent += copies

    def s0(self):
        return [self.copy(0, self.g.at[1 - self.at.c], self.r0, self.at.at_c())]

    def rows_y(self, d, h):
        return self.g.at[self.at.c, lax.rem(self.at.y + d, NY), pl.ds(2 * h, 2)]

    def rows_x(self, d, h):
        return self.g.at[self.at.c, :, pl.ds(4 + 2 * h, 2), lax.rem(self.at.x + d, NX)]

    def s1_pass(self):
        at = self.at
        return [
            self.copy(1, self.rows_y(2, 0), self.r1p.at[0, 0], at.at_y(1)),
            self.copy(2, self.rows_y(2, 1), self.r1p.at[0, 1], at.at_y(3)),
            self.copy(3, self.rows_x(2, 0), self.r1q.at[0, 0], at.at_x(1)),
            self.copy(4, self.rows_x(2, 1), self.r1q.at[0, 1], at.at_x(3)),
        ]

    def s1_direct(self):
        at = self.at
        return [
            self.copy(5, self.rows_y(1, 1), self.r1p.at[1, 1], at.at_y(1)),
            self.copy(6, self.rows_y(3, 0), self.r1p.at[1, 0], at.at_y(3)),
            self.copy(7, self.rows_x(1, 1), self.r1q.at[1, 1], at.at_x(1)),
            self.copy(8, self.rows_x(3, 0), self.r1q.at[1, 0], at.at_x(3)),
        ]

    def s1_on(self):
        at = self.at
        return [
            self.copy(9, self.rows_y(1, 0), self.r1p.at[2, 0], at.at_y(1)),
            self.copy(10, self.rows_y(3, 1), self.r1p.at[2, 1], at.at_y(3)),
            self.copy(11, self.rows_x(1, 0), self.r1q.at[2, 0], at.at_x(1)),
            self.copy(12, self.rows_x(3, 1), self.r1q.at[2, 1], at.at_x(3)),
        ]

    def s2(self):
        at, out = self.at, []
        for d in (1, 3, 2):
            y = lax.rem(at.y + d, NY)
            x = lax.rem(at.x + d, NX)
            out.append(self.copy(12 + d, self.a1p.at[:, x], self.r2p.at[d - 1], at.at_x(d)))
            out.append(self.copy(15 + d, self.a1q.at[y], self.r2q.at[d - 1], at.at_y(d)))
        return out

    def s3(self):
        at, out = self.at, []
        for d in (1, 7, 2, 6, 3, 5, 4):
            z = lax.rem(at.z + d, NZ)
            out.append(self.copy(18 + d, self.a2.at[z], self.r3.at[d - 1], at.at_z(d)))
        return out

    def s4(self):
        at, out = self.at, []
        mine = at.c * NY + at.y
        for d in range(1, 8):
            out.append(self.copy(25 + d, self.fin.at[mine], self.fin.at[mine], at.at_dp(d)))
        return out

    def arrived(self, copies):
        for one in copies:
            one.wait_recv()

    def start(self):
        self.go(self.s0())

    def over_core(self):
        self.arrived(self.s0())
        c = self.at.c

        def add(y):
            self.g[c, y] = (self.g[c, y].astype(F32) + self.r0[y].astype(F32)).astype(BF)

        loop(NY, add)
        self.go(self.s1_pass() + self.s1_direct())

    def pass_on(self):
        self.arrived(self.s1_pass())
        for h, d in ((0, 1), (1, 3)):
            rows = self.rows_y(d, h)
            rows[...] = (rows[...].astype(F32) + self.r1p[0, h].astype(F32)).astype(BF)
            rows = self.rows_x(d, h)
            rows[...] = (rows[...].astype(F32) + self.r1q[0, h].astype(F32)).astype(BF)
        self.go(self.s1_on())

    def over_first(self):
        self.arrived(self.s1_direct() + self.s1_on())
        for h in range(2):
            total = self.rows_y(0, h)[...].astype(F32) + self.r1p[1, h].astype(F32)
            self.a1p[pl.ds(2 * h, 2)] = (total + self.r1p[2, h].astype(F32)).astype(BF)
            total = self.rows_x(0, h)[...].astype(F32) + self.r1q[1, h].astype(F32)
            self.a1q[:, pl.ds(2 * h, 2)] = (total + self.r1q[2, h].astype(F32)).astype(BF)
        self.go(self.s2())

    def over_second(self):
        self.arrived(self.s2())
        y, x = self.at.y, self.at.x

        def add(i):
            total = self.a1p[i, x].astype(F32)
            other = self.a1q[y, i].astype(F32)
            for d in range(3):
                total = total + self.r2p[d, i].astype(F32)
                other = other + self.r2q[d, i].astype(F32)
            self.a2[i] = total.astype(BF)
            self.a2[4 + i] = other.astype(BF)

        loop(4, add)
        self.go(self.s3())

    def over_z(self, factor):
        self.arrived(self.s3())
        total = self.a2[self.at.z].astype(F32)
        for d in range(7):
            total = total + self.r3[d].astype(F32)
        self.fin[self.at.c * NY + self.at.y] = (total * factor).astype(BF)
        self.go(self.s4())

    def gathered(self):
        self.arrived(self.s4())

    def close(self):
        for one in self.sent:
            one.wait_send()


def kernel(
    lengths, route, rows_grad, h_conv_pre, h_conv_in, h_conv_w, h_proj_w, h_in_w, depth_w, depth_gain,
    h_out_w,
    o_input, o_fin_out, o_fin_in, o_fin_rest,
    outgoing, incoming, pre, cin_halo, linked, seg, act, slope, feat, linear, sigma, glu, mixed,
    swish_t, dfac, inv, dmix, up, hot, taps, gainsum, dj, df, dpre, feat_t, act_t, sel_t, pairs, dgs, shifts,
    conv_in, conv_w, proj_w, in_w, out_w, load_sem,
    a2a_send, a2a_recv, halo_send, halo_recv,
    *parts_refs,
):
    at = Place()
    tm = at.tm
    p_out, p_in, p_rest = (Part(at, parts_refs[13 * i : 13 * i + 13]) for i in range(3))
    left, right = (at.dp, lax.rem(tm + NTM - 1, NTM)), (at.dp, lax.rem(tm + 1, NTM))

    loads = [
        pltpu.make_async_copy(src, dst, load_sem.at[i])
        for i, (src, dst) in enumerate(
            (
                (h_conv_pre, pre.at[pl.ds(H, F)]),
                (h_conv_in, conv_in),
                (h_proj_w, proj_w),
                (h_in_w, in_w),
                (h_out_w, out_w),
                (h_conv_w, conv_w),
            )
        )
    ]
    for one in loads:
        one.start()

    barrier = pltpu.get_barrier_semaphore()

    def greet(d):
        pl.semaphore_signal(barrier, inc=1, device_id=at.at_tm(d + 1), device_id_type=MESH)

    loop(NTM - 1, greet)
    for d in range(1, 8):
        pl.semaphore_signal(barrier, inc=1, device_id=at.at_dp(d), device_id_type=MESH)

    order = route[...]
    owner_row = lax.div(order, F).astype(F32)
    local_row = lax.rem(order, F).astype(F32) + 1.0
    sub = lax.broadcasted_iota(jnp.int32, (F, F), 0)
    lane = lax.broadcasted_iota(jnp.int32, (F, F), 1)
    owners = jnp.broadcast_to(owner_row, (F, F))
    owner_col = jnp.sum(jnp.where(sub == lane, owners, 0.0), axis=1, keepdims=True)
    local_col = jnp.sum(
        jnp.where(sub == lane, jnp.broadcast_to(local_row, (F, F)), 0.0), axis=1, keepdims=True
    )
    before = jnp.where((owners == owner_col) & (sub < lane), 1.0, 0.0)
    slot_row = owner_row * CAP + jnp.sum(before, axis=0, keepdims=True)
    slots = lax.broadcasted_iota(jnp.int32, (NTM * CAP, F), 0).astype(F32)
    hot[...] = jnp.where(slots == slot_row, 1.0, 0.0).astype(BF)

    def pack(j):
        outgoing[:, block(j, 256)] = dot(hot[...], rows_grad[:, block(j, 256)]).astype(BF)

    loop(4, pack)
    outgoing[:, D : D + IDX] = dot(
        hot[...], jnp.broadcast_to(local_col, (F, IDX)).astype(BF)
    ).astype(BF)

    pl.semaphore_wait(barrier, NTM - 1 + 7)

    for one in loads[:2]:
        one.wait()
    halos = [
        remote(pre.at[pl.ds(H, H)], pre.at[pl.ds(H + F, H)], halo_send.at[0], halo_recv.at[0], left),
        remote(pre.at[pl.ds(F, H)], pre.at[pl.ds(0, H)], halo_send.at[1], halo_recv.at[1], right),
        remote(conv_in.at[pl.ds(2 * F - 16, 16)], cin_halo, halo_send.at[2], halo_recv.at[2], right),
    ]
    for one in halos:
        one.start()

    def routed(d):
        other = lax.rem(tm + d, NTM)
        return remote(
            outgoing.at[block(other, CAP)],
            incoming.at[block(tm, CAP)],
            a2a_send.at[d],
            a2a_recv.at[d],
            (at.dp, other),
        )

    loop(NTM - 1, lambda d: routed(d + 1).start())
    incoming[block(tm, CAP)] = outgoing[block(tm, CAP)]

    bound0 = lengths[0, 0]
    bound1 = bound0 + lengths[0, 1]
    bound2 = bound1 + lengths[0, 2]
    bound3 = bound2 + lengths[0, 3]
    pos = tm * F - H + lax.broadcasted_iota(jnp.int32, (PAD, 128), 0)
    number = sum((pos >= b).astype(jnp.int32) for b in (bound0, bound1, bound2, bound3))
    inside = (pos >= 0) & (pos < F * NTM)
    seg[...] = jnp.where(inside, number, -1)
    for k in range(KW):
        linked[k] = jnp.where(seg[pl.ds(H + k - HALF, NEXT)] == seg[pl.ds(H, NEXT)], 1.0, 0.0)
    taps[pl.ds(0, KW), :] = depth_w[...].astype(F32)
    glu[pl.ds(EXT, 8), :] = jnp.zeros((8, D), F32)
    dmix[pl.ds(EXT, 8), :] = jnp.zeros((8, D), F32)
    dj[pl.ds(F, 16), :] = jnp.zeros((16, 2 * D), BF)

    for one in loads[2:4]:
        one.wait()
    for one in halos[:2]:
        one.wait_recv()

    def gelu(i):
        rows = block(i, 32)
        v = pre[rows, :].astype(F32)
        half = 0.5 * (1.0 + lax.erf(v * (1.0 / math.sqrt(2.0))))
        act[rows, :] = (v * half).astype(BF)
        slope[rows, :] = half + v * jnp.exp(-0.5 * v * v) * (1.0 / math.sqrt(2.0 * math.pi))

    loop(EXT // 32, gelu)

    def features(j):
        feat[:, block(j, 256)] = dot(act[...], proj_w[:, block(j, 256)]).astype(BF)

    loop(4, features)

    def joined(j):
        lin = dot(feat[...], in_w[:, block(j, 256)])
        sig = jax.nn.sigmoid(dot(feat[...], in_w[:, block(4 + j, 256)]))
        linear[:, block(j, 256)] = lin
        sigma[:, block(j, 256)] = sig
        glu[pl.ds(0, EXT), block(j, 256)] = (lin * sig).astype(BF).astype(F32)

    loop(4, joined)

    def mix(j):
        cols = block(j, 128)
        shift_all(shifts, glu, cols)
        for r in range(0, F, 64):
            total = jnp.zeros((64, 128), F32)
            for k in range(KW):
                rows = shifted(shifts, k, r, 64)
                total = total + taps[pl.ds(k, 1), cols] * (rows * linked[k, pl.ds(r, 64)])
            mixed[pl.ds(r, 64), cols] = total

    loop(8, mix)
    gain = depth_gain[...].astype(F32).reshape(1, D)

    def norm_all(i):
        rows = block(i, 32)
        v = mixed[rows, :]
        v = v - jnp.mean(v, axis=1, keepdims=True)
        scale = 1.0 / jnp.sqrt(jnp.mean(v * v, axis=1, keepdims=True) + EPS)
        v = v * scale
        inv[rows, :] = jnp.broadcast_to(scale, (32, 128))
        mixed[rows, :] = v
        scaled = v * gain
        s = jax.nn.sigmoid(scaled)
        dfac[rows, :] = s * (1.0 + scaled * (1.0 - s))
        dmix[pl.ds(pl.multiple_of(H + i * 32, 16), 32), :] = scaled * s

    loop(8, norm_all)

    def turn(j):
        cols = block(j, 256)
        swish_t[cols, :] = jnp.transpose(dmix[pl.ds(H, F), cols]).astype(BF)
        feat_t[cols, :] = jnp.transpose(feat[pl.ds(H, F), cols].astype(F32)).astype(BF)

    loop(4, turn)

    def turn_act(j):
        cols = block(j, 256)
        act_t[cols, :] = jnp.transpose(act[pl.ds(H, F), cols].astype(F32)).astype(BF)

    loop(2, turn_act)

    halos[2].wait_recv()
    r_f = lax.broadcasted_iota(jnp.int32, (F, 2 * F), 0)
    c_f = lax.broadcasted_iota(jnp.int32, (F, 2 * F), 1)
    r_h = lax.broadcasted_iota(jnp.int32, (F, 16), 0)
    c_h = lax.broadcasted_iota(jnp.int32, (F, 16), 1)
    first = (r_h == 0) & (c_h == 15) & (tm > 0)

    def one_hot(mask):
        return jnp.where(mask, 1.0, 0.0).astype(BF)

    for tap in range(3):
        rows = dot(one_hot(c_f == 2 * r_f + tap - 1), conv_in[...])
        if tap == 0:
            rows = rows + dot(one_hot(first), cin_halo[...])
        pairs[tap] = jnp.transpose(rows).astype(BF)

    loop(NTM - 1, lambda d: routed(d + 1).wait_recv())
    number = incoming[:, D : D + IDX].astype(F32)
    number = jnp.concatenate([number, number], axis=1)
    wanted = lax.broadcasted_iota(jnp.int32, (NTM * CAP, F), 1).astype(F32) + 1.0
    chosen = jnp.where(number == wanted, 1.0, 0.0)
    sel_t[...] = jnp.transpose(chosen).astype(BF)

    def place(j):
        up[pl.ds(0, F), block(j, 256)] = dot(sel_t[...], incoming[:, block(j, 256)]).astype(BF)

    loop(4, place)
    edge_up = remote(up.at[pl.ds(0, 16)], up.at[pl.ds(F, 16)], halo_send.at[3], halo_recv.at[3], left)
    edge_up.start()

    for one in loads[4:]:
        one.wait()

    def dswish(j):
        cols = block(j, 256)
        dfac[:, cols] = dfac[:, cols] * dot_nt(up[pl.ds(0, F), :], out_w[block(j, 256), :])

    loop(4, dswish)
    gainsum[...] = jnp.zeros((8, D), F32)

    def dnorm(i):
        rows = block(i, 32)
        ds = dfac[rows, :]
        v = mixed[rows, :]
        dv = ds * v
        gainsum[...] += dv[0:8] + dv[8:16] + dv[16:24] + dv[24:32]
        q = ds * gain
        q = q - jnp.mean(q, axis=1, keepdims=True) - v * jnp.mean(q * v, axis=1, keepdims=True)
        dmix[pl.ds(pl.multiple_of(H + i * 32, 16), 32), :] = inv[rows, pl.ds(0, 1)] * q

    loop(8, dnorm)
    edges = [
        remote(dmix.at[pl.ds(H, H)], dmix.at[pl.ds(H + F, H)], halo_send.at[4], halo_recv.at[4], left),
        remote(dmix.at[pl.ds(F, H)], dmix.at[pl.ds(0, H)], halo_send.at[5], halo_recv.at[5], right),
    ]
    for one in edges:
        one.start()

    def out_terms(half):
        def body(i):
            b = half * 2 + i
            cols = block(b, 256)
            term = dot(swish_t[...], up[pl.ds(0, F), cols]).astype(BF)
            for s in range(2):
                y = i * 2 + s
                p_out.g[half, y] = term[:, 128 * s : 128 * s + 128].reshape(NZ, NX, 32, 128)

        loop(2, body)

    out_terms(1 - at.c)
    p_out.start()
    out_terms(at.c)
    p_out.over_core()

    for one in edges:
        one.wait_recv()
    edge_up.wait_recv()

    def dconv(j):
        cols = block(j, 128)
        gates = block(8 + j, 128)
        shift_all(shifts, dmix, cols)
        for r, size in ((0, 64), (64, 64), (128, 64), (192, 64), (256, 8)):
            total = jnp.zeros((size, 128), F32)
            for k in range(KW):
                rows = shifted(shifts, k, r, size)
                total = total + taps[pl.ds(KW - 1 - k, 1), cols] * (
                    rows * linked[k, pl.ds(r, size)]
                )
            sig = sigma[pl.ds(H + r, size), cols]
            ds = total * sig
            dg = ds * linear[pl.ds(H + r, size), cols] * (1.0 - sig)
            if size == 8:
                zero = jnp.zeros((8, 128), F32)
                ds = jnp.concatenate([ds, zero], axis=0)
                dg = jnp.concatenate([dg, zero], axis=0)
            dj[pl.ds(r, max(size, 16)), cols] = ds.astype(BF)
            dj[pl.ds(r, max(size, 16)), gates] = dg.astype(BF)

    loop(4, dconv)
    p_out.pass_on()
    loop(4, lambda j: dconv(4 + j))

    def in_terms(half):
        def body(y):
            term = dot(feat_t[...], dj[pl.ds(0, F), block(half * 4 + y, 256)]).astype(BF)
            for s in range(2):
                p_in.g[half, y, :, :, pl.ds(32 * s, 32), :] = term[
                    :, 128 * s : 128 * s + 128
                ].reshape(NZ, NX, 32, 128)

        loop(4, body)

    in_terms(1 - at.c)
    p_in.start()
    in_terms(at.c)
    p_out.over_first()

    def dfeatures(j):
        cols = block(j, 256)
        df[:, cols] = (up[:, cols].astype(F32) + dot_nt(dj[...], in_w[cols, :])).astype(BF)

    loop(4, dfeatures)
    p_in.over_core()

    def dpres(j):
        cols = block(j, 256)
        dpre[:, cols] = (dot_nt(df[...], proj_w[cols, :]) * slope[pl.ds(H, NEXT16), cols]).astype(BF)

    loop(2, dpres)

    def rest_terms(half):
        def body(i):
            cols = block(half * 2 + i, 256)
            term = dot(act_t[...], df[pl.ds(0, F), cols]).astype(BF)
            for s in range(2):
                y = i * 2 + s
                p_rest.g[half, y, :, :, pl.ds(0, 16), :] = term[
                    :, 128 * s : 128 * s + 128
                ].reshape(NZ, NX, 16, 128)

        loop(2, body)

    def conv_terms(tap, core, row):
        def body(i):
            term = dot(pairs[tap], dpre[pl.ds(0, F), block(i, 256)]).astype(BF)
            for s in range(2):
                p_rest.g[core, i * 2 + s, :, :, pl.ds(row, 16), :] = term[
                    :, 128 * s : 128 * s + 128
                ].reshape(NZ, NX, 16, 128)

        loop(2, body)

    rest_terms(0)
    rest_terms(1)
    p_in.pass_on()
    for tap, core, row in ((0, 0, 16), (1, 0, 32), (2, 1, 16)):
        conv_terms(tap, core, row)
    p_out.over_second()

    def depth(j):
        cols = block(j, 128)
        shift_all(shifts, glu, cols)
        total = [None] * KW
        for r in range(0, F, 64):
            grad = dmix[pl.ds(H + r, 64), cols]
            for k in range(KW):
                rows = shifted(shifts, k, r, 64)
                term = jnp.sum((rows * linked[k, pl.ds(r, 64)] * grad).reshape(8, 8, 128), axis=0)
                total[k] = term if r == 0 else total[k] + term
        for k in range(KW):
            dgs[k // 8, pl.ds(k % 8, 1), cols] = jnp.sum(total[k], axis=0, keepdims=True)

    dgs[:, pl.ds(8, 8), :] = jnp.zeros((4, 8, D), F32)
    loop(8, depth)
    dgs[3, pl.ds(7, 1), :] = jnp.sum(gainsum[...], axis=0, keepdims=True)
    p_in.over_first()
    for z in range(NZ):
        small = dgs[:, :, 128 * z : 128 * z + 128].astype(BF)
        for x in range(NX):
            p_rest.g[1, :, z, x, pl.ds(32, 16), :] = small
    p_rest.start()

    factor = 1.0 / math.sqrt(F * NTM * 8)
    p_out.over_z(factor)

    r_o = lax.broadcasted_iota(jnp.int32, (2 * F, NEXT16), 0)
    c_o = lax.broadcasted_iota(jnp.int32, (2 * F, NEXT16), 1)
    here = dot(one_hot(r_o == 2 * c_o), dpre[...]).astype(BF)
    here_odd = dot(one_hot(r_o == 2 * c_o + 1), dpre[...]).astype(BF)
    ahead = (r_o == 2 * c_o - 1) & ((c_o < F) | (tm < NTM - 1))
    ahead = dot(one_hot(ahead), dpre[...]).astype(BF)
    o_input[...] = dot_nt(here, conv_w[1])
    o_input[...] += dot_nt(here_odd, conv_w[2])
    o_input[...] += dot_nt(ahead, conv_w[0])

    p_rest.over_core()
    p_in.over_second()
    p_rest.pass_on()
    p_in.over_z(factor)
    p_rest.over_first()
    p_out.gathered()
    o_fin_out[...] = p_out.fin[...]
    p_rest.over_second()
    p_in.gathered()
    o_fin_in[...] = p_in.fin[...]
    p_rest.over_z(factor)
    p_rest.gathered()
    o_fin_rest[...] = p_rest.fin[...]

    loop(NTM - 1, lambda d: routed(d + 1).wait_send())
    for one in halos + [edge_up] + edges:
        one.wait_send()
    for part in (p_out, p_in, p_rest):
        part.close()


def spread(
    rows, f_out, f_in, f_rest, o_input, o_conv, o_proj, o_in, o_depth, o_gain, o_out, done
):
    whole = pltpu.make_async_copy(rows, o_input, done)
    whole.start()
    for b in range(8):
        cols = pl.ds(128 * b, 128)
        o_out[:, cols] = f_out[b].astype(F32)
        o_proj[:, cols] = f_rest[b, pl.ds(0, 16)].astype(F32)
        for s in range(2):
            o_in[:, pl.ds(256 * b + 128 * s, 128)] = f_in[b, pl.ds(32 * s, 32)].astype(F32)
    x = lax.rem(lax.axis_index("tm"), NX)
    for y in range(NY):
        cols = pl.ds(128 * y, 128)
        o_conv[0, :, cols] = f_rest[y, pl.ds(16, 16)].astype(F32)
        o_conv[1, :, cols] = f_rest[y, pl.ds(32, 16)].astype(F32)
        o_conv[2, :, cols] = f_rest[NY + y, pl.ds(16, 16)].astype(F32)
        small = f_rest[NY + y, pl.ds(32, 16)].astype(F32)[0:8]
        mine = jnp.zeros((8, 32), F32)
        for other in range(NX):
            mine = mine + jnp.where(x == other, small[:, 32 * other : 32 * other + 32], 0.0)
        if y < NY - 1:
            o_depth[pl.ds(8 * y, 8), :] = mine
        else:
            o_depth[pl.ds(8 * y, 7), :] = mine[0:7]
            o_gain[...] = mine[7:8]
    whole.wait()


def per_device(
    grad_attn, route, lengths, conv_pre, conv_in, conv_w, proj_w, in_w, depth_w, depth_gain, out_w
):
    vmem = pl.BlockSpec(memory_space=pltpu.VMEM)
    anywhere = pl.BlockSpec(memory_space=pl.ANY)
    smem = pl.BlockSpec(memory_space=pltpu.SMEM)
    scratch = [
        pltpu.VMEM((NTM * CAP, D + IDX), BF),
        pltpu.VMEM((NTM * CAP, D + IDX), BF),
        pltpu.VMEM((EXT, CF), BF),
        pltpu.VMEM((16, CF), BF),
        pltpu.VMEM((KW, NEXT, 128), F32),
        pltpu.VMEM((PAD, 128), jnp.int32),
        pltpu.VMEM((EXT, CF), BF),
        pltpu.VMEM((EXT, CF), F32),
        pltpu.VMEM((EXT, D), BF),
        pltpu.VMEM((EXT, D), F32),
        pltpu.VMEM((EXT, D), F32),
        pltpu.VMEM((PAD, D), F32),
        pltpu.VMEM((F, D), F32),
        pltpu.VMEM((D, F), BF),
        pltpu.VMEM((F, D), F32),
        pltpu.VMEM((F, 128), F32),
        pltpu.VMEM((PAD, D), F32),
        pltpu.VMEM((NEXT16, D), BF),
        pltpu.VMEM((NTM * CAP, F), BF),
        pltpu.VMEM((32, D), F32),
        pltpu.VMEM((8, D), F32),
        pltpu.VMEM((NEXT16, 2 * D), BF),
        pltpu.VMEM((NEXT16, D), BF),
        pltpu.VMEM((NEXT16, CF), BF),
        pltpu.VMEM((D, F), BF),
        pltpu.VMEM((CF, F), BF),
        pltpu.VMEM((F, NTM * CAP), BF),
        pltpu.VMEM((3, CF, F), BF),
        pltpu.VMEM((4, 16, D), F32),
        pltpu.VMEM((8, EXT, 128), F32),
        pltpu.VMEM((2 * F, CF), BF),
        pltpu.VMEM((3, CF, CF), BF),
        pltpu.VMEM((CF, D), BF),
        pltpu.VMEM((D, 2 * D), BF),
        pltpu.VMEM((D, D), BF),
        pltpu.SemaphoreType.DMA((6,)),
        pltpu.SemaphoreType.DMA((NTM,)),
        pltpu.SemaphoreType.DMA((NTM,)),
        pltpu.SemaphoreType.DMA((6,)),
        pltpu.SemaphoreType.DMA((6,)),
    ]
    for rows in PART_ROWS:
        scratch += part_scratch(rows)
    outs = pl.pallas_call(
        kernel,
        out_shape=[jax.ShapeDtypeStruct((2 * F, CF), F32)]
        + [jax.ShapeDtypeStruct((8, rows, 128), BF) for rows in PART_ROWS],
        in_specs=[smem] + [vmem] * 2 + [anywhere] * 5 + [vmem] * 2 + [anywhere],
        out_specs=[vmem] * 4,
        scratch_shapes=scratch,
        compiler_params=pltpu.CompilerParams(
            collective_id=0, has_side_effects=True, vmem_limit_bytes=62 * 2**20
        ),
    )(
        lengths, route, grad_attn[0], conv_pre[0], conv_in[0], conv_w, proj_w, in_w, depth_w,
        depth_gain, out_w,
    )
    o_input, o_conv, o_proj, o_in, o_depth, o_gain, o_out = pl.pallas_call(
        spread,
        out_shape=[
            jax.ShapeDtypeStruct((2 * F, CF), F32),
            jax.ShapeDtypeStruct((3, 16, CF), F32),
            jax.ShapeDtypeStruct((16, D), F32),
            jax.ShapeDtypeStruct((32, 2 * D), F32),
            jax.ShapeDtypeStruct((KW, 32), F32),
            jax.ShapeDtypeStruct((1, 32), F32),
            jax.ShapeDtypeStruct((32, D), F32),
        ],
        in_specs=[vmem] * 4,
        out_specs=[anywhere] + [vmem] * 6,
        scratch_shapes=[pltpu.SemaphoreType.DMA],
    )(*outs)
    return (o_input[None], o_conv, o_proj, o_in, o_depth, o_gain[0], o_out)


def solution(mesh):
    placed = (
        P("dp", "tm", None),
        P("dp", "tm"),
        P("dp", None),
        P("dp", "tm", None),
        P("dp", "tm", None),
        P(),
        P(),
        P(),
        P(),
        P(),
        P(),
    )
    return jax.shard_map(
        per_device,
        mesh=mesh,
        in_specs=placed,
        out_specs=(
            P("dp", "tm", None),
            P(None, "tm", None),
            P("tm", None),
            P("tm", None),
            P(None, "tm"),
            P("tm"),
            P("tm", None),
        ),
        check_vma=False,
    )
```

```python
import functools
import math

import jax
import jax.numpy as jnp
from jax import lax
from jax.experimental import pallas as pl
from jax.experimental.pallas import tpu as pltpu
from jax.sharding import PartitionSpec as P

EPS = 1e-05
MESH = pl.DeviceIdType.MESH
BF, F32 = jnp.bfloat16, jnp.float32

F = 256
D = 1024
CF = 512
KW = 31
HALF = 15
H = 16
EXT = F + 2 * H
PAD = EXT + 8
NEXT = F + 8
NEXT16 = F + 16
CAP = 16
NTM, NZ, NX, NY, NC = 32, 8, 4, 4, 2
IDX = 128
PART_ROWS = (32, 64, 48)

NT = (((1,), (1,)), ((), ()))


def dot(a, b):
    return jnp.dot(a, b, preferred_element_type=F32)


def dot_nt(a, b):
    return lax.dot_general(a, b, NT, preferred_element_type=F32)


def block(i, size):
    return pl.ds(pl.multiple_of(i * size, size), size)


def loop(n, body):
    def step(i, carry):
        body(i)
        return carry

    lax.fori_loop(0, n, step, 0)


def shift_all(shifts, ref, cols):
    for shift in range(8):
        shifts[shift] = ref[pl.ds(H - HALF + shift, EXT), cols]


def shifted(shifts, tap, start, size):
    return shifts[tap % 8, pl.ds(start + tap - tap % 8, size)]


class Place:
    def __init__(self):
        self.dp = lax.axis_index("dp")
        self.tm = lax.axis_index("tm")
        self.y = lax.div(self.dp, 2)
        self.c = lax.rem(self.dp, 2)
        self.z = lax.div(self.tm, NX)
        self.x = lax.rem(self.tm, NX)

    def at_c(self):
        return (self.y * 2 + (1 - self.c), self.tm)

    def at_y(self, d):
        return (lax.rem(self.y + d, NY) * 2 + self.c, self.tm)

    def at_x(self, d):
        return (self.dp, self.z * NX + lax.rem(self.x + d, NX))

    def at_z(self, d):
        return (self.dp, lax.rem(self.z + d, NZ) * NX + self.x)

    def at_dp(self, d):
        return (lax.rem(self.dp + d, 8), self.tm)

    def at_tm(self, d):
        return (self.dp, lax.rem(self.tm + d, NTM))


def remote(src, dst, send, recv, device):
    return pltpu.make_async_remote_copy(
        src_ref=src, dst_ref=dst, send_sem=send, recv_sem=recv, device_id=device, device_id_type=MESH
    )


def part_scratch(rows):
    tile = (rows, 128)
    return [
        pltpu.VMEM((NC, NY, NZ, NX) + tile, BF),
        pltpu.VMEM((NY, NZ, NX) + tile, BF),
        pltpu.VMEM((3, 2, 2, NX) + tile, BF),
        pltpu.VMEM((3, 2, NY, 2) + tile, BF),
        pltpu.VMEM((4, NX) + tile, BF),
        pltpu.VMEM((NY, 4) + tile, BF),
        pltpu.VMEM((3, 4) + tile, BF),
        pltpu.VMEM((3, 4) + tile, BF),
        pltpu.VMEM((NZ,) + tile, BF),
        pltpu.VMEM((7,) + tile, BF),
        pltpu.VMEM((8,) + tile, BF),
        pltpu.SemaphoreType.DMA((33,)),
        pltpu.SemaphoreType.DMA((33,)),
    ]


class Part:
    def __init__(self, at, refs):
        self.at = at
        (self.g, self.r0, self.r1p, self.r1q, self.a1p, self.a1q, self.r2p, self.r2q) = refs[:8]
        (self.a2, self.r3, self.fin, self.send, self.recv) = refs[8:]
        self.sent = []

    def copy(self, i, src, dst, device):
        return remote(src, dst, self.send.at[i], self.recv.at[i], device)

    def go(self, copies):
        for one in copies:
            one.start()
        self.sent += copies

    def s0(self):
        return [self.copy(0, self.g.at[1 - self.at.c], self.r0, self.at.at_c())]

    def rows_y(self, d, h):
        return self.g.at[self.at.c, lax.rem(self.at.y + d, NY), pl.ds(2 * h, 2)]

    def rows_x(self, d, h):
        return self.g.at[self.at.c, :, pl.ds(4 + 2 * h, 2), lax.rem(self.at.x + d, NX)]

    def s1_pass(self):
        at = self.at
        return [
            self.copy(1, self.rows_y(2, 0), self.r1p.at[0, 0], at.at_y(1)),
            self.copy(2, self.rows_y(2, 1), self.r1p.at[0, 1], at.at_y(3)),
            self.copy(3, self.rows_x(2, 0), self.r1q.at[0, 0], at.at_x(1)),
            self.copy(4, self.rows_x(2, 1), self.r1q.at[0, 1], at.at_x(3)),
        ]

    def s1_direct(self):
        at = self.at
        return [
            self.copy(5, self.rows_y(1, 1), self.r1p.at[1, 1], at.at_y(1)),
            self.copy(6, self.rows_y(3, 0), self.r1p.at[1, 0], at.at_y(3)),
            self.copy(7, self.rows_x(1, 1), self.r1q.at[1, 1], at.at_x(1)),
            self.copy(8, self.rows_x(3, 0), self.r1q.at[1, 0], at.at_x(3)),
        ]

    def s1_on(self):
        at = self.at
        return [
            self.copy(9, self.rows_y(1, 0), self.r1p.at[2, 0], at.at_y(1)),
            self.copy(10, self.rows_y(3, 1), self.r1p.at[2, 1], at.at_y(3)),
            self.copy(11, self.rows_x(1, 0), self.r1q.at[2, 0], at.at_x(1)),
            self.copy(12, self.rows_x(3, 1), self.r1q.at[2, 1], at.at_x(3)),
        ]

    def s2(self):
        at, out = self.at, []
        for d in (1, 3, 2):
            y = lax.rem(at.y + d, NY)
            x = lax.rem(at.x + d, NX)
            out.append(self.copy(12 + d, self.a1p.at[:, x], self.r2p.at[d - 1], at.at_x(d)))
            out.append(self.copy(15 + d, self.a1q.at[y], self.r2q.at[d - 1], at.at_y(d)))
        return out

    def s3(self):
        at, out = self.at, []
        for d in (1, 7, 2, 6, 3, 5, 4):
            z = lax.rem(at.z + d, NZ)
            out.append(self.copy(18 + d, self.a2.at[z], self.r3.at[d - 1], at.at_z(d)))
        return out

    def s4(self):
        at, out = self.at, []
        mine = at.c * NY + at.y
        for d in range(1, 8):
            out.append(self.copy(25 + d, self.fin.at[mine], self.fin.at[mine], at.at_dp(d)))
        return out

    def arrived(self, copies):
        for one in copies:
            one.wait_recv()

    def start(self):
        self.go(self.s0())

    def over_core(self):
        self.arrived(self.s0())
        c = self.at.c

        def add(y):
            self.g[c, y] = self.g[c, y] + self.r0[y]

        loop(NY, add)
        self.go(self.s1_pass() + self.s1_direct())

    def pass_on(self):
        self.arrived(self.s1_pass())
        for h, d in ((0, 1), (1, 3)):
            rows = self.rows_y(d, h)
            rows[...] = rows[...] + self.r1p[0, h]
            rows = self.rows_x(d, h)
            rows[...] = rows[...] + self.r1q[0, h]
        self.go(self.s1_on())

    def over_first(self):
        self.arrived(self.s1_direct() + self.s1_on())
        for h in range(2):
            total = self.rows_y(0, h)[...].astype(F32) + self.r1p[1, h].astype(F32)
            self.a1p[pl.ds(2 * h, 2)] = (total + self.r1p[2, h].astype(F32)).astype(BF)
            total = self.rows_x(0, h)[...].astype(F32) + self.r1q[1, h].astype(F32)
            self.a1q[:, pl.ds(2 * h, 2)] = (total + self.r1q[2, h].astype(F32)).astype(BF)
        self.go(self.s2())

    def over_second(self, join=None):
        self.arrived(self.s2())
        y, x = self.at.y, self.at.x

        def add(i):
            total = self.a1p[i, x].astype(F32)
            other = self.a1q[y, i].astype(F32)
            for d in range(3):
                total = total + self.r2p[d, i].astype(F32)
                other = other + self.r2q[d, i].astype(F32)
            self.a2[i] = total.astype(BF)
            self.a2[4 + i] = other.astype(BF)

        loop(4, add)
        if join is not None:
            join(self.a2)
        self.go(self.s3())

    def over_z(self, factor):
        self.arrived(self.s3())
        total = self.a2[self.at.z].astype(F32)
        for d in range(7):
            total = total + self.r3[d].astype(F32)
        self.fin[self.at.c * NY + self.at.y] = (total * factor).astype(BF)
        self.go(self.s4())

    def gathered(self):
        self.arrived(self.s4())

    def close(self):
        for one in self.sent:
            one.wait_send()


class Small(Part):
    def __init__(self, at, refs):
        self.at = at
        self.own, self.core, self.from_y, self.some, self.from_x, self.send, self.recv = refs
        self.sent = []

    def over_y(self):
        return [
            self.copy(
                d, self.own.at[lax.rem(self.at.y + d, NY)], self.from_y.at[d - 1], self.at.at_y(d)
            )
            for d in range(1, 4)
        ]

    def over_x(self):
        return [
            self.copy(3 + d, self.some, self.from_x.at[d - 1], self.at.at_x(d)) for d in range(1, 4)
        ]

    def s0(self):
        return [self.copy(0, self.own, self.core, self.at.at_c())]

    def begin(self, terms):
        self.own[...] = terms[...].astype(BF)
        self.go(self.s0())

    def second(self):
        self.arrived(self.s0())
        for one in self.s0():
            one.wait_send()
        self.sent = []
        self.own[...] = self.own[...] + self.core[...]
        self.go(self.over_y())

    def total(self, first, others):
        total = first.astype(F32)
        for d in range(3):
            total = total + others[d].astype(F32)
        return total.astype(BF)

    def third(self):
        self.arrived(self.over_y())
        self.some[...] = self.total(self.own[self.at.y], self.from_y)
        self.go(self.over_x())

    def join(self, sums):
        self.arrived(self.over_x())
        total = self.total(self.some[...], self.from_x).astype(F32)
        for z in range(NZ):
            there = sums[z, pl.ds(32, 16)].astype(F32)
            mine = total[:, 128 * z : 128 * z + 128]
            sums[z, pl.ds(32, 16)] = jnp.where(self.at.c == 1, mine, there).astype(BF)


def kernel(
    lengths, route, rows_grad, h_conv_pre, h_conv_in, h_conv_w, h_proj_w, h_in_w, depth_w, depth_gain,
    h_out_w,
    o_input, o_fin_out, o_fin_in, o_fin_rest,
    outgoing, incoming, pre, cin_halo, linked, seg, act, slope, feat, linear, sigma, glu, mixed,
    swish_t, dfac, inv, dmix, up, hot, taps, gainsum, dj, df, dpre, feat_t, act_t, sel_t, pairs, dgs, shifts,
    conv_in, conv_w, proj_w, in_w, out_w, load_sem,
    a2a_send, a2a_recv, halo_send, halo_recv,
    *parts_refs,
):
    at = Place()
    tm = at.tm
    p_out, p_in, p_rest = (Part(at, parts_refs[13 * i : 13 * i + 13]) for i in range(3))
    p_small = Small(at, parts_refs[39:])
    left, right = (at.dp, lax.rem(tm + NTM - 1, NTM)), (at.dp, lax.rem(tm + 1, NTM))

    loads = [
        pltpu.make_async_copy(src, dst, load_sem.at[i])
        for i, (src, dst) in enumerate(
            (
                (h_conv_pre, pre.at[pl.ds(H, F)]),
                (h_conv_in, conv_in),
                (h_proj_w, proj_w),
                (h_in_w, in_w),
                (h_out_w, out_w),
                (h_conv_w, conv_w),
            )
        )
    ]
    for one in loads:
        one.start()

    barrier = pltpu.get_barrier_semaphore()

    def greet(d):
        pl.semaphore_signal(barrier, inc=1, device_id=at.at_tm(d + 1), device_id_type=MESH)

    loop(NTM - 1, greet)
    for d in range(1, 8):
        pl.semaphore_signal(barrier, inc=1, device_id=at.at_dp(d), device_id_type=MESH)

    order = route[...]
    owner_row = lax.div(order, F).astype(F32)
    local_row = lax.rem(order, F).astype(F32) + 1.0
    sub = lax.broadcasted_iota(jnp.int32, (F, F), 0)
    lane = lax.broadcasted_iota(jnp.int32, (F, F), 1)
    owners = jnp.broadcast_to(owner_row, (F, F))
    owner_col = jnp.sum(jnp.where(sub == lane, owners, 0.0), axis=1, keepdims=True)
    local_col = jnp.sum(
        jnp.where(sub == lane, jnp.broadcast_to(local_row, (F, F)), 0.0), axis=1, keepdims=True
    )
    before = jnp.where((owners == owner_col) & (sub < lane), 1.0, 0.0)
    slot_row = owner_row * CAP + jnp.sum(before, axis=0, keepdims=True)
    slots = lax.broadcasted_iota(jnp.int32, (NTM * CAP, F), 0).astype(F32)
    hot[...] = jnp.where(slots == slot_row, 1.0, 0.0).astype(BF)

    def pack(j):
        outgoing[:, block(j, 256)] = dot(hot[...], rows_grad[:, block(j, 256)]).astype(BF)

    loop(4, pack)
    outgoing[:, D : D + IDX] = dot(
        hot[...], jnp.broadcast_to(local_col, (F, IDX)).astype(BF)
    ).astype(BF)

    pl.semaphore_wait(barrier, NTM - 1 + 7)

    for one in loads[:2]:
        one.wait()
    halos = [
        remote(pre.at[pl.ds(H, H)], pre.at[pl.ds(H + F, H)], halo_send.at[0], halo_recv.at[0], left),
        remote(pre.at[pl.ds(F, H)], pre.at[pl.ds(0, H)], halo_send.at[1], halo_recv.at[1], right),
        remote(conv_in.at[pl.ds(2 * F - 16, 16)], cin_halo, halo_send.at[2], halo_recv.at[2], right),
    ]
    for one in halos:
        one.start()

    def routed(d):
        other = lax.rem(tm + d, NTM)
        return remote(
            outgoing.at[block(other, CAP)],
            incoming.at[block(tm, CAP)],
            a2a_send.at[d],
            a2a_recv.at[d],
            (at.dp, other),
        )

    loop(NTM - 1, lambda d: routed(d + 1).start())
    incoming[block(tm, CAP)] = outgoing[block(tm, CAP)]

    bound0 = lengths[0, 0]
    bound1 = bound0 + lengths[0, 1]
    bound2 = bound1 + lengths[0, 2]
    bound3 = bound2 + lengths[0, 3]
    pos = tm * F - H + lax.broadcasted_iota(jnp.int32, (PAD, 128), 0)
    number = sum((pos >= b).astype(jnp.int32) for b in (bound0, bound1, bound2, bound3))
    inside = (pos >= 0) & (pos < F * NTM)
    seg[...] = jnp.where(inside, number, -1)
    for k in range(KW):
        linked[k] = jnp.where(seg[pl.ds(H + k - HALF, NEXT)] == seg[pl.ds(H, NEXT)], 1.0, 0.0)
    taps[pl.ds(0, KW), :] = depth_w[...].astype(F32)
    glu[pl.ds(EXT, 8), :] = jnp.zeros((8, D), F32)
    dmix[pl.ds(EXT, 8), :] = jnp.zeros((8, D), F32)
    dj[pl.ds(F, 16), :] = jnp.zeros((16, 2 * D), BF)
    dgs[:, pl.ds(8, 8), :] = jnp.zeros((4, 8, D), F32)
    for y in range(NY):
        p_rest.g[1, y, :, :, pl.ds(32, 16), :] = jnp.zeros((NZ, NX, 16, 128), BF)

    for one in loads[2:4]:
        one.wait()
    for one in halos[:2]:
        one.wait_recv()

    def gelu(i):
        rows = block(i, 32)
        v = pre[rows, :].astype(F32)
        half = 0.5 * (1.0 + lax.erf(v * (1.0 / math.sqrt(2.0))))
        act[rows, :] = (v * half).astype(BF)
        slope[rows, :] = half + v * jnp.exp(-0.5 * v * v) * (1.0 / math.sqrt(2.0 * math.pi))

    loop(EXT // 32, gelu)

    def features(j):
        feat[:, block(j, 256)] = dot(act[...], proj_w[:, block(j, 256)]).astype(BF)

    loop(4, features)

    def joined(j):
        lin = dot(feat[...], in_w[:, block(j, 256)])
        sig = jax.nn.sigmoid(dot(feat[...], in_w[:, block(4 + j, 256)]))
        linear[:, block(j, 256)] = lin
        sigma[:, block(j, 256)] = sig
        glu[pl.ds(0, EXT), block(j, 256)] = (lin * sig).astype(BF).astype(F32)

    loop(4, joined)

    def mix(j):
        cols = block(j, 128)
        shift_all(shifts, glu, cols)
        for r in range(0, F, 64):
            total = jnp.zeros((64, 128), F32)
            for k in range(KW):
                rows = shifted(shifts, k, r, 64)
                total = total + taps[pl.ds(k, 1), cols] * (rows * linked[k, pl.ds(r, 64)])
            mixed[pl.ds(r, 64), cols] = total

    loop(8, mix)
    gain = depth_gain[...].astype(F32).reshape(1, D)

    def norm_all(i):
        rows = block(i, 32)
        v = mixed[rows, :]
        v = v - jnp.mean(v, axis=1, keepdims=True)
        scale = 1.0 / jnp.sqrt(jnp.mean(v * v, axis=1, keepdims=True) + EPS)
        v = v * scale
        inv[rows, :] = jnp.broadcast_to(scale, (32, 128))
        mixed[rows, :] = v
        scaled = v * gain
        s = jax.nn.sigmoid(scaled)
        dfac[rows, :] = s * (1.0 + scaled * (1.0 - s))
        dmix[pl.ds(pl.multiple_of(H + i * 32, 16), 32), :] = scaled * s

    loop(8, norm_all)

    def turn(j):
        cols = block(j, 256)
        swish_t[cols, :] = jnp.transpose(dmix[pl.ds(H, F), cols]).astype(BF)
        feat_t[cols, :] = jnp.transpose(feat[pl.ds(H, F), cols].astype(F32)).astype(BF)

    loop(4, turn)

    def turn_act(j):
        cols = block(j, 256)
        act_t[cols, :] = jnp.transpose(act[pl.ds(H, F), cols].astype(F32)).astype(BF)

    loop(2, turn_act)

    halos[2].wait_recv()
    r_f = lax.broadcasted_iota(jnp.int32, (F, 2 * F), 0)
    c_f = lax.broadcasted_iota(jnp.int32, (F, 2 * F), 1)
    r_h = lax.broadcasted_iota(jnp.int32, (F, 16), 0)
    c_h = lax.broadcasted_iota(jnp.int32, (F, 16), 1)
    first = (r_h == 0) & (c_h == 15) & (tm > 0)

    def one_hot(mask):
        return jnp.where(mask, 1.0, 0.0).astype(BF)

    for tap in range(3):
        rows = dot(one_hot(c_f == 2 * r_f + tap - 1), conv_in[...])
        if tap == 0:
            rows = rows + dot(one_hot(first), cin_halo[...])
        pairs[tap] = jnp.transpose(rows).astype(BF)

    loop(NTM - 1, lambda d: routed(d + 1).wait_recv())
    number = incoming[:, D : D + IDX].astype(F32)
    number = jnp.concatenate([number, number], axis=1)
    wanted = lax.broadcasted_iota(jnp.int32, (NTM * CAP, F), 1).astype(F32) + 1.0
    chosen = jnp.where(number == wanted, 1.0, 0.0)
    sel_t[...] = jnp.transpose(chosen).astype(BF)

    def place(j):
        up[pl.ds(0, F), block(j, 256)] = dot(sel_t[...], incoming[:, block(j, 256)]).astype(BF)

    loop(4, place)
    edge_up = remote(up.at[pl.ds(0, 16)], up.at[pl.ds(F, 16)], halo_send.at[3], halo_recv.at[3], left)
    edge_up.start()

    for one in loads[4:]:
        one.wait()

    def dswish(j):
        cols = block(j, 256)
        dfac[:, cols] = dfac[:, cols] * dot_nt(up[pl.ds(0, F), :], out_w[block(j, 256), :])

    loop(4, dswish)
    gainsum[...] = jnp.zeros((8, D), F32)

    def dnorm(i):
        rows = block(i, 32)
        ds = dfac[rows, :]
        v = mixed[rows, :]
        dv = ds * v
        gainsum[...] += dv[0:8] + dv[8:16] + dv[16:24] + dv[24:32]
        q = ds * gain
        q = q - jnp.mean(q, axis=1, keepdims=True) - v * jnp.mean(q * v, axis=1, keepdims=True)
        dmix[pl.ds(pl.multiple_of(H + i * 32, 16), 32), :] = inv[rows, pl.ds(0, 1)] * q

    loop(8, dnorm)
    edges = [
        remote(dmix.at[pl.ds(H, H)], dmix.at[pl.ds(H + F, H)], halo_send.at[4], halo_recv.at[4], left),
        remote(dmix.at[pl.ds(F, H)], dmix.at[pl.ds(0, H)], halo_send.at[5], halo_recv.at[5], right),
    ]
    for one in edges:
        one.start()

    def out_terms(half):
        def body(i):
            b = half * 2 + i
            cols = block(b, 256)
            term = dot(swish_t[...], up[pl.ds(0, F), cols]).astype(BF)
            for s in range(2):
                y = i * 2 + s
                p_out.g[half, y] = term[:, 128 * s : 128 * s + 128].reshape(NZ, NX, 32, 128)

        loop(2, body)

    out_terms(1 - at.c)
    p_out.start()
    out_terms(at.c)

    def depth(j):
        cols = block(j, 128)
        shift_all(shifts, glu, cols)
        total = [None] * KW
        for r in range(0, F, 64):
            grad = dmix[pl.ds(H + r, 64), cols]
            for k in range(KW):
                rows = shifted(shifts, k, r, 64)
                term = jnp.sum((rows * linked[k, pl.ds(r, 64)] * grad).reshape(8, 8, 128), axis=0)
                total[k] = term if r == 0 else total[k] + term
        for k in range(KW):
            dgs[k // 8, pl.ds(k % 8, 1), cols] = jnp.sum(total[k], axis=0, keepdims=True)

    p_out.over_core()

    for one in edges:
        one.wait_recv()
    edge_up.wait_recv()

    def dconv(j):
        cols = block(j, 128)
        gates = block(8 + j, 128)
        shift_all(shifts, dmix, cols)
        for r, size in ((0, 64), (64, 64), (128, 64), (192, 64), (256, 8)):
            total = jnp.zeros((size, 128), F32)
            for k in range(KW):
                rows = shifted(shifts, k, r, size)
                total = total + taps[pl.ds(KW - 1 - k, 1), cols] * (
                    rows * linked[k, pl.ds(r, size)]
                )
            sig = sigma[pl.ds(H + r, size), cols]
            ds = total * sig
            dg = ds * linear[pl.ds(H + r, size), cols] * (1.0 - sig)
            if size == 8:
                zero = jnp.zeros((8, 128), F32)
                ds = jnp.concatenate([ds, zero], axis=0)
                dg = jnp.concatenate([dg, zero], axis=0)
            dj[pl.ds(r, max(size, 16)), cols] = ds.astype(BF)
            dj[pl.ds(r, max(size, 16)), gates] = dg.astype(BF)

    loop(4, dconv)
    p_out.pass_on()
    loop(4, lambda j: dconv(4 + j))

    def in_terms(half):
        def body(y):
            term = dot(feat_t[...], dj[pl.ds(0, F), block(half * 4 + y, 256)]).astype(BF)
            for s in range(2):
                p_in.g[half, y, :, :, pl.ds(32 * s, 32), :] = term[
                    :, 128 * s : 128 * s + 128
                ].reshape(NZ, NX, 32, 128)

        loop(4, body)

    in_terms(1 - at.c)
    p_in.start()
    in_terms(at.c)
    p_out.over_first()

    def dfeatures(j):
        cols = block(j, 256)
        df[:, cols] = (up[:, cols].astype(F32) + dot_nt(dj[...], in_w[cols, :])).astype(BF)

    loop(4, dfeatures)
    p_in.over_core()

    def dpres(j):
        cols = block(j, 256)
        dpre[:, cols] = (dot_nt(df[...], proj_w[cols, :]) * slope[pl.ds(H, NEXT16), cols]).astype(BF)

    loop(2, dpres)

    def rest_terms(half):
        def body(i):
            cols = block(half * 2 + i, 256)
            term = dot(act_t[...], df[pl.ds(0, F), cols]).astype(BF)
            for s in range(2):
                y = i * 2 + s
                p_rest.g[half, y, :, :, pl.ds(0, 16), :] = term[
                    :, 128 * s : 128 * s + 128
                ].reshape(NZ, NX, 16, 128)

        loop(2, body)

    def conv_terms(tap, core, row):
        def body(i):
            term = dot(pairs[tap], dpre[pl.ds(0, F), block(i, 256)]).astype(BF)
            for s in range(2):
                p_rest.g[core, i * 2 + s, :, :, pl.ds(row, 16), :] = term[
                    :, 128 * s : 128 * s + 128
                ].reshape(NZ, NX, 16, 128)

        loop(2, body)

    rest_terms(0)
    rest_terms(1)
    for tap, core, row in ((0, 0, 16), (1, 0, 32), (2, 1, 16)):
        conv_terms(tap, core, row)
    p_rest.start()
    p_out.over_second()
    loop(2, depth)
    p_in.pass_on()
    p_rest.over_core()
    loop(3, lambda j: depth(2 + j))
    p_in.over_first()
    p_rest.pass_on()
    loop(3, lambda j: depth(5 + j))
    dgs[3, pl.ds(7, 1), :] = jnp.sum(gainsum[...], axis=0, keepdims=True)
    p_small.begin(dgs)
    factor = 1.0 / math.sqrt(F * NTM * 8)
    p_out.over_z(factor)

    r_o = lax.broadcasted_iota(jnp.int32, (2 * F, NEXT16), 0)
    c_o = lax.broadcasted_iota(jnp.int32, (2 * F, NEXT16), 1)
    here = dot(one_hot(r_o == 2 * c_o), dpre[...]).astype(BF)
    here_odd = dot(one_hot(r_o == 2 * c_o + 1), dpre[...]).astype(BF)
    ahead = (r_o == 2 * c_o - 1) & ((c_o < F) | (tm < NTM - 1))
    ahead = dot(one_hot(ahead), dpre[...]).astype(BF)
    o_input[...] = dot_nt(here, conv_w[1])
    o_input[...] += dot_nt(here_odd, conv_w[2])
    o_input[...] += dot_nt(ahead, conv_w[0])

    p_small.second()
    p_in.over_second()
    p_rest.over_first()
    p_small.third()
    p_in.over_z(factor)
    p_rest.over_second(p_small.join)
    p_out.gathered()
    o_fin_out[...] = p_out.fin[...]
    p_in.gathered()
    o_fin_in[...] = p_in.fin[...]
    p_rest.over_z(factor)
    p_rest.gathered()
    o_fin_rest[...] = p_rest.fin[...]

    loop(NTM - 1, lambda d: routed(d + 1).wait_send())
    for one in halos + [edge_up] + edges:
        one.wait_send()
    for part in (p_out, p_in, p_rest, p_small):
        part.close()


def spread(
    rows, f_out, f_in, f_rest, o_input, o_conv, o_proj, o_in, o_depth, o_gain, o_out, done
):
    whole = pltpu.make_async_copy(rows, o_input, done)
    whole.start()
    for b in range(8):
        cols = pl.ds(128 * b, 128)
        o_out[:, cols] = f_out[b].astype(F32)
        o_proj[:, cols] = f_rest[b, pl.ds(0, 16)].astype(F32)
        for s in range(2):
            o_in[:, pl.ds(256 * b + 128 * s, 128)] = f_in[b, pl.ds(32 * s, 32)].astype(F32)
    x = lax.rem(lax.axis_index("tm"), NX)
    for y in range(NY):
        cols = pl.ds(128 * y, 128)
        o_conv[0, :, cols] = f_rest[y, pl.ds(16, 16)].astype(F32)
        o_conv[1, :, cols] = f_rest[y, pl.ds(32, 16)].astype(F32)
        o_conv[2, :, cols] = f_rest[NY + y, pl.ds(16, 16)].astype(F32)
        small = f_rest[NY + y, pl.ds(32, 16)].astype(F32)[0:8]
        mine = jnp.zeros((8, 32), F32)
        for other in range(NX):
            mine = mine + jnp.where(x == other, small[:, 32 * other : 32 * other + 32], 0.0)
        if y < NY - 1:
            o_depth[pl.ds(8 * y, 8), :] = mine
        else:
            o_depth[pl.ds(8 * y, 7), :] = mine[0:7]
            o_gain[...] = mine[7:8]
    whole.wait()


def per_device(
    grad_attn, route, lengths, conv_pre, conv_in, conv_w, proj_w, in_w, depth_w, depth_gain, out_w
):
    vmem = pl.BlockSpec(memory_space=pltpu.VMEM)
    anywhere = pl.BlockSpec(memory_space=pl.ANY)
    smem = pl.BlockSpec(memory_space=pltpu.SMEM)
    scratch = [
        pltpu.VMEM((NTM * CAP, D + IDX), BF),
        pltpu.VMEM((NTM * CAP, D + IDX), BF),
        pltpu.VMEM((EXT, CF), BF),
        pltpu.VMEM((16, CF), BF),
        pltpu.VMEM((KW, NEXT, 128), F32),
        pltpu.VMEM((PAD, 128), jnp.int32),
        pltpu.VMEM((EXT, CF), BF),
        pltpu.VMEM((EXT, CF), F32),
        pltpu.VMEM((EXT, D), BF),
        pltpu.VMEM((EXT, D), F32),
        pltpu.VMEM((EXT, D), F32),
        pltpu.VMEM((PAD, D), F32),
        pltpu.VMEM((F, D), F32),
        pltpu.VMEM((D, F), BF),
        pltpu.VMEM((F, D), F32),
        pltpu.VMEM((F, 128), F32),
        pltpu.VMEM((PAD, D), F32),
        pltpu.VMEM((NEXT16, D), BF),
        pltpu.VMEM((NTM * CAP, F), BF),
        pltpu.VMEM((32, D), F32),
        pltpu.VMEM((8, D), F32),
        pltpu.VMEM((NEXT16, 2 * D), BF),
        pltpu.VMEM((NEXT16, D), BF),
        pltpu.VMEM((NEXT16, CF), BF),
        pltpu.VMEM((D, F), BF),
        pltpu.VMEM((CF, F), BF),
        pltpu.VMEM((F, NTM * CAP), BF),
        pltpu.VMEM((3, CF, F), BF),
        pltpu.VMEM((4, 16, D), F32),
        pltpu.VMEM((8, EXT, 128), F32),
        pltpu.VMEM((2 * F, CF), BF),
        pltpu.VMEM((3, CF, CF), BF),
        pltpu.VMEM((CF, D), BF),
        pltpu.VMEM((D, 2 * D), BF),
        pltpu.VMEM((D, D), BF),
        pltpu.SemaphoreType.DMA((6,)),
        pltpu.SemaphoreType.DMA((NTM,)),
        pltpu.SemaphoreType.DMA((NTM,)),
        pltpu.SemaphoreType.DMA((6,)),
        pltpu.SemaphoreType.DMA((6,)),
    ]
    for rows in PART_ROWS:
        scratch += part_scratch(rows)
    scratch += [
        pltpu.VMEM((NY, 16, D), BF),
        pltpu.VMEM((NY, 16, D), BF),
        pltpu.VMEM((3, 16, D), BF),
        pltpu.VMEM((16, D), BF),
        pltpu.VMEM((3, 16, D), BF),
        pltpu.SemaphoreType.DMA((7,)),
        pltpu.SemaphoreType.DMA((7,)),
    ]
    outs = pl.pallas_call(
        kernel,
        out_shape=[jax.ShapeDtypeStruct((2 * F, CF), F32)]
        + [jax.ShapeDtypeStruct((8, rows, 128), BF) for rows in PART_ROWS],
        in_specs=[smem] + [vmem] * 2 + [anywhere] * 5 + [vmem] * 2 + [anywhere],
        out_specs=[vmem] * 4,
        scratch_shapes=scratch,
        compiler_params=pltpu.CompilerParams(
            collective_id=0, has_side_effects=True, vmem_limit_bytes=62 * 2**20
        ),
    )(
        lengths, route, grad_attn[0], conv_pre[0], conv_in[0], conv_w, proj_w, in_w, depth_w,
        depth_gain, out_w,
    )
    o_input, o_conv, o_proj, o_in, o_depth, o_gain, o_out = pl.pallas_call(
        spread,
        out_shape=[
            jax.ShapeDtypeStruct((2 * F, CF), F32),
            jax.ShapeDtypeStruct((3, 16, CF), F32),
            jax.ShapeDtypeStruct((16, D), F32),
            jax.ShapeDtypeStruct((32, 2 * D), F32),
            jax.ShapeDtypeStruct((KW, 32), F32),
            jax.ShapeDtypeStruct((1, 32), F32),
            jax.ShapeDtypeStruct((32, D), F32),
        ],
        in_specs=[vmem] * 4,
        out_specs=[anywhere] + [vmem] * 6,
        scratch_shapes=[pltpu.SemaphoreType.DMA],
    )(*outs)
    return (o_input[None], o_conv, o_proj, o_in, o_depth, o_gain[0], o_out)


def solution(mesh):
    placed = (
        P("dp", "tm", None),
        P("dp", "tm"),
        P("dp", None),
        P("dp", "tm", None),
        P("dp", "tm", None),
        P(),
        P(),
        P(),
        P(),
        P(),
        P(),
    )
    return jax.shard_map(
        per_device,
        mesh=mesh,
        in_specs=placed,
        out_specs=(
            P("dp", "tm", None),
            P(None, "tm", None),
            P("tm", None),
            P("tm", None),
            P(None, "tm"),
            P("tm"),
            P("tm", None),
        ),
        check_vma=False,
    )
```

```python
import functools
import math

import jax
import jax.numpy as jnp
from jax import lax
from jax.experimental import pallas as pl
from jax.experimental.pallas import tpu as pltpu
from jax.sharding import PartitionSpec as P

EPS = 1e-05
MESH = pl.DeviceIdType.MESH
BF, F32 = jnp.bfloat16, jnp.float32

F = 256
D = 1024
CF = 512
KW = 31
HALF = 15
H = 16
EXT = F + 2 * H
PAD = EXT + 8
NEXT = F + 8
NEXT16 = F + 16
CAP = 16
NTM, NZ, NX, NY, NC = 32, 8, 4, 4, 2
IDX = 128
PART_ROWS = (32, 64, 48)

NT = (((1,), (1,)), ((), ()))


def dot(a, b):
    return jnp.dot(a, b, preferred_element_type=F32)


def dot_nt(a, b):
    return lax.dot_general(a, b, NT, preferred_element_type=F32)


def block(i, size):
    return pl.ds(pl.multiple_of(i * size, size), size)


def loop(n, body):
    def step(i, carry):
        body(i)
        return carry

    lax.fori_loop(0, n, step, 0)


def shift_all(shifts, ref, cols):
    for shift in range(8):
        shifts[shift] = ref[pl.ds(H - HALF + shift, EXT), cols]


def shifted(shifts, tap, start, size):
    return shifts[tap % 8, pl.ds(start + tap - tap % 8, size)]


class Place:
    def __init__(self):
        self.dp = lax.axis_index("dp")
        self.tm = lax.axis_index("tm")
        self.y = lax.div(self.dp, 2)
        self.c = lax.rem(self.dp, 2)
        self.z = lax.div(self.tm, NX)
        self.x = lax.rem(self.tm, NX)

    def at_c(self):
        return (self.y * 2 + (1 - self.c), self.tm)

    def at_y(self, d):
        return (lax.rem(self.y + d, NY) * 2 + self.c, self.tm)

    def at_x(self, d):
        return (self.dp, self.z * NX + lax.rem(self.x + d, NX))

    def at_z(self, d):
        return (self.dp, lax.rem(self.z + d, NZ) * NX + self.x)

    def at_dp(self, d):
        return (lax.rem(self.dp + d, 8), self.tm)

    def at_tm(self, d):
        return (self.dp, lax.rem(self.tm + d, NTM))


def remote(src, dst, send, recv, device):
    return pltpu.make_async_remote_copy(
        src_ref=src, dst_ref=dst, send_sem=send, recv_sem=recv, device_id=device, device_id_type=MESH
    )


def part_scratch(rows):
    tile = (rows, 128)
    return [
        pltpu.VMEM((NC, NY, NZ, NX) + tile, BF),
        pltpu.VMEM((NY, NZ, NX) + tile, BF),
        pltpu.VMEM((3, 2, 2, NX) + tile, BF),
        pltpu.VMEM((3, 2, NY, 2) + tile, BF),
        pltpu.VMEM((4, NX) + tile, BF),
        pltpu.VMEM((NY, 4) + tile, BF),
        pltpu.VMEM((3, 4) + tile, BF),
        pltpu.VMEM((3, 4) + tile, BF),
        pltpu.VMEM((NZ,) + tile, BF),
        pltpu.VMEM((7,) + tile, BF),
        pltpu.VMEM((8,) + tile, BF),
        pltpu.SemaphoreType.DMA((33,)),
        pltpu.SemaphoreType.DMA((33,)),
    ]


class Part:
    def __init__(self, at, refs):
        self.at = at
        (self.g, self.r0, self.r1p, self.r1q, self.a1p, self.a1q, self.r2p, self.r2q) = refs[:8]
        (self.a2, self.r3, self.fin, self.send, self.recv) = refs[8:]
        self.sent = []

    def copy(self, i, src, dst, device):
        return remote(src, dst, self.send.at[i], self.recv.at[i], device)

    def go(self, copies):
        for one in copies:
            one.start()
        self.sent += copies

    def s0(self):
        return [self.copy(0, self.g.at[1 - self.at.c], self.r0, self.at.at_c())]

    def rows_y(self, d, h):
        return self.g.at[self.at.c, lax.rem(self.at.y + d, NY), pl.ds(2 * h, 2)]

    def rows_x(self, d, h):
        return self.g.at[self.at.c, :, pl.ds(4 + 2 * h, 2), lax.rem(self.at.x + d, NX)]

    def s1_pass(self):
        at = self.at
        return [
            self.copy(1, self.rows_y(2, 0), self.r1p.at[0, 0], at.at_y(1)),
            self.copy(2, self.rows_y(2, 1), self.r1p.at[0, 1], at.at_y(3)),
            self.copy(3, self.rows_x(2, 0), self.r1q.at[0, 0], at.at_x(1)),
            self.copy(4, self.rows_x(2, 1), self.r1q.at[0, 1], at.at_x(3)),
        ]

    def s1_direct(self):
        at = self.at
        return [
            self.copy(5, self.rows_y(1, 1), self.r1p.at[1, 1], at.at_y(1)),
            self.copy(6, self.rows_y(3, 0), self.r1p.at[1, 0], at.at_y(3)),
            self.copy(7, self.rows_x(1, 1), self.r1q.at[1, 1], at.at_x(1)),
            self.copy(8, self.rows_x(3, 0), self.r1q.at[1, 0], at.at_x(3)),
        ]

    def s1_on(self):
        at = self.at
        return [
            self.copy(9, self.rows_y(1, 0), self.r1p.at[2, 0], at.at_y(1)),
            self.copy(10, self.rows_y(3, 1), self.r1p.at[2, 1], at.at_y(3)),
            self.copy(11, self.rows_x(1, 0), self.r1q.at[2, 0], at.at_x(1)),
            self.copy(12, self.rows_x(3, 1), self.r1q.at[2, 1], at.at_x(3)),
        ]

    def s2(self):
        at, out = self.at, []
        for d in (1, 3, 2):
            y = lax.rem(at.y + d, NY)
            x = lax.rem(at.x + d, NX)
            out.append(self.copy(12 + d, self.a1p.at[:, x], self.r2p.at[d - 1], at.at_x(d)))
            out.append(self.copy(15 + d, self.a1q.at[y], self.r2q.at[d - 1], at.at_y(d)))
        return out

    def s3(self):
        at, out = self.at, []
        for d in (1, 7, 2, 6, 3, 5, 4):
            z = lax.rem(at.z + d, NZ)
            out.append(self.copy(18 + d, self.a2.at[z], self.r3.at[d - 1], at.at_z(d)))
        return out

    def s4(self):
        at, out = self.at, []
        mine = at.c * NY + at.y
        for d in range(1, 8):
            out.append(self.copy(25 + d, self.fin.at[mine], self.fin.at[mine], at.at_dp(d)))
        return out

    def arrived(self, copies):
        for one in copies:
            one.wait_recv()

    def start(self):
        self.go(self.s0())

    def over_core(self):
        self.arrived(self.s0())
        c = self.at.c

        def add(y):
            self.g[c, y] = self.g[c, y] + self.r0[y]

        loop(NY, add)
        self.go(self.s1_pass() + self.s1_direct())

    def pass_on(self):
        self.arrived(self.s1_pass())
        for h, d in ((0, 1), (1, 3)):
            rows = self.rows_y(d, h)
            rows[...] = rows[...] + self.r1p[0, h]
            rows = self.rows_x(d, h)
            rows[...] = rows[...] + self.r1q[0, h]
        self.go(self.s1_on())

    def over_first(self):
        self.arrived(self.s1_direct() + self.s1_on())
        for h in range(2):
            total = self.rows_y(0, h)[...].astype(F32) + self.r1p[1, h].astype(F32)
            self.a1p[pl.ds(2 * h, 2)] = (total + self.r1p[2, h].astype(F32)).astype(BF)
            total = self.rows_x(0, h)[...].astype(F32) + self.r1q[1, h].astype(F32)
            self.a1q[:, pl.ds(2 * h, 2)] = (total + self.r1q[2, h].astype(F32)).astype(BF)
        self.go(self.s2())

    def over_second(self, join=None):
        self.arrived(self.s2())
        y, x = self.at.y, self.at.x

        def add(i):
            total = self.a1p[i, x].astype(F32)
            other = self.a1q[y, i].astype(F32)
            for d in range(3):
                total = total + self.r2p[d, i].astype(F32)
                other = other + self.r2q[d, i].astype(F32)
            self.a2[i] = total.astype(BF)
            self.a2[4 + i] = other.astype(BF)

        loop(4, add)
        if join is not None:
            join(self.a2)
        self.go(self.s3())

    def over_z(self, factor):
        self.arrived(self.s3())
        total = self.a2[self.at.z].astype(F32)
        for d in range(7):
            total = total + self.r3[d].astype(F32)
        self.fin[self.at.c * NY + self.at.y] = (total * factor).astype(BF)
        self.go(self.s4())

    def gathered(self):
        self.arrived(self.s4())

    def close(self):
        for one in self.sent:
            one.wait_send()


class Small(Part):
    def __init__(self, at, refs):
        self.at = at
        self.own, self.core, self.from_y, self.some, self.from_x, self.send, self.recv = refs
        self.sent = []

    def over_y(self):
        return [
            self.copy(
                d, self.own.at[lax.rem(self.at.y + d, NY)], self.from_y.at[d - 1], self.at.at_y(d)
            )
            for d in range(1, 4)
        ]

    def over_x(self):
        return [
            self.copy(3 + d, self.some, self.from_x.at[d - 1], self.at.at_x(d)) for d in range(1, 4)
        ]

    def s0(self):
        return [self.copy(0, self.own, self.core, self.at.at_c())]

    def begin(self, terms):
        self.own[...] = terms[...].astype(BF)
        self.go(self.s0())

    def second(self):
        self.arrived(self.s0())
        for one in self.s0():
            one.wait_send()
        self.sent = []
        self.own[...] = self.own[...] + self.core[...]
        self.go(self.over_y())

    def total(self, first, others):
        total = first.astype(F32)
        for d in range(3):
            total = total + others[d].astype(F32)
        return total.astype(BF)

    def third(self):
        self.arrived(self.over_y())
        self.some[...] = self.total(self.own[self.at.y], self.from_y)
        self.go(self.over_x())

    def join(self, sums):
        self.arrived(self.over_x())
        total = self.total(self.some[...], self.from_x).astype(F32)
        for z in range(NZ):
            there = sums[z, pl.ds(32, 16)].astype(F32)
            mine = total[:, 128 * z : 128 * z + 128]
            sums[z, pl.ds(32, 16)] = jnp.where(self.at.c == 1, mine, there).astype(BF)


def kernel(
    lengths, route, rows_grad, h_conv_pre, h_conv_in, h_conv_w, h_proj_w, h_in_w, depth_w, depth_gain,
    h_out_w,
    o_input, o_fin_out, o_fin_in, o_fin_rest,
    outgoing, incoming, pre, cin_halo, linked, seg, act, slope, feat, linear, sigma, glu, mixed,
    swish_t, dfac, inv, dmix, up, hot, taps, gainsum, dj, df, dpre, feat_t, act_t, sel_t, pairs, dgs, shifts,
    conv_in, conv_w, proj_w, in_w, out_w, load_sem,
    a2a_send, a2a_recv, halo_send, halo_recv,
    *parts_refs,
):
    at = Place()
    tm = at.tm
    p_out, p_in, p_rest = (Part(at, parts_refs[13 * i : 13 * i + 13]) for i in range(3))
    p_small = Small(at, parts_refs[39:])
    left, right = (at.dp, lax.rem(tm + NTM - 1, NTM)), (at.dp, lax.rem(tm + 1, NTM))

    loads = [
        pltpu.make_async_copy(src, dst, load_sem.at[i])
        for i, (src, dst) in enumerate(
            (
                (h_conv_pre, pre.at[pl.ds(H, F)]),
                (h_conv_in, conv_in),
                (h_proj_w, proj_w),
                (h_in_w, in_w),
                (h_out_w, out_w),
                (h_conv_w, conv_w),
            )
        )
    ]
    for one in loads:
        one.start()

    barrier = pltpu.get_barrier_semaphore()

    def greet(d):
        pl.semaphore_signal(barrier, inc=1, device_id=at.at_tm(d + 1), device_id_type=MESH)

    loop(NTM - 1, greet)
    for d in range(1, 8):
        pl.semaphore_signal(barrier, inc=1, device_id=at.at_dp(d), device_id_type=MESH)

    order = route[...]
    owner_row = lax.div(order, F).astype(F32)
    local_row = lax.rem(order, F).astype(F32) + 1.0
    sub = lax.broadcasted_iota(jnp.int32, (F, F), 0)
    lane = lax.broadcasted_iota(jnp.int32, (F, F), 1)
    owners = jnp.broadcast_to(owner_row, (F, F))
    owner_col = jnp.sum(jnp.where(sub == lane, owners, 0.0), axis=1, keepdims=True)
    local_col = jnp.sum(
        jnp.where(sub == lane, jnp.broadcast_to(local_row, (F, F)), 0.0), axis=1, keepdims=True
    )
    before = jnp.where((owners == owner_col) & (sub < lane), 1.0, 0.0)
    slot_row = owner_row * CAP + jnp.sum(before, axis=0, keepdims=True)
    slots = lax.broadcasted_iota(jnp.int32, (NTM * CAP, F), 0).astype(F32)
    hot[...] = jnp.where(slots == slot_row, 1.0, 0.0).astype(BF)

    def pack(j):
        outgoing[:, block(j, 256)] = dot(hot[...], rows_grad[:, block(j, 256)]).astype(BF)

    loop(4, pack)
    outgoing[:, D : D + IDX] = dot(
        hot[...], jnp.broadcast_to(local_col, (F, IDX)).astype(BF)
    ).astype(BF)

    pl.semaphore_wait(barrier, NTM - 1 + 7)

    for one in loads[:2]:
        one.wait()
    halos = [
        remote(pre.at[pl.ds(H, H)], pre.at[pl.ds(H + F, H)], halo_send.at[0], halo_recv.at[0], left),
        remote(pre.at[pl.ds(F, H)], pre.at[pl.ds(0, H)], halo_send.at[1], halo_recv.at[1], right),
        remote(conv_in.at[pl.ds(2 * F - 16, 16)], cin_halo, halo_send.at[2], halo_recv.at[2], right),
    ]
    for one in halos:
        one.start()

    def routed(d):
        other = lax.rem(tm + d, NTM)
        return remote(
            outgoing.at[block(other, CAP)],
            incoming.at[block(tm, CAP)],
            a2a_send.at[d],
            a2a_recv.at[d],
            (at.dp, other),
        )

    def both_ways(i):
        near = lax.div(i, 2) + 1
        routed(jnp.where(lax.rem(i, 2) == 0, near, NTM - near)).start()

    loop(NTM - 1, both_ways)
    incoming[block(tm, CAP)] = outgoing[block(tm, CAP)]

    bound0 = lengths[0, 0]
    bound1 = bound0 + lengths[0, 1]
    bound2 = bound1 + lengths[0, 2]
    bound3 = bound2 + lengths[0, 3]
    pos = tm * F - H + lax.broadcasted_iota(jnp.int32, (PAD, 128), 0)
    number = sum((pos >= b).astype(jnp.int32) for b in (bound0, bound1, bound2, bound3))
    inside = (pos >= 0) & (pos < F * NTM)
    seg[...] = jnp.where(inside, number, -1)
    for k in range(KW):
        linked[k] = jnp.where(seg[pl.ds(H + k - HALF, NEXT)] == seg[pl.ds(H, NEXT)], 1.0, 0.0)
    taps[pl.ds(0, KW), :] = depth_w[...].astype(F32)
    glu[pl.ds(EXT, 8), :] = jnp.zeros((8, D), F32)
    dmix[pl.ds(EXT, 8), :] = jnp.zeros((8, D), F32)
    dj[pl.ds(F, 16), :] = jnp.zeros((16, 2 * D), BF)
    dgs[:, pl.ds(8, 8), :] = jnp.zeros((4, 8, D), F32)
    for y in range(NY):
        p_rest.g[1, y, :, :, pl.ds(32, 16), :] = jnp.zeros((NZ, NX, 16, 128), BF)

    for one in loads[2:4]:
        one.wait()
    for one in halos[:2]:
        one.wait_recv()

    def gelu(i):
        rows = block(i, 32)
        v = pre[rows, :].astype(F32)
        half = 0.5 * (1.0 + lax.erf(v * (1.0 / math.sqrt(2.0))))
        act[rows, :] = (v * half).astype(BF)
        slope[rows, :] = half + v * jnp.exp(-0.5 * v * v) * (1.0 / math.sqrt(2.0 * math.pi))

    loop(EXT // 32, gelu)

    def features(j):
        feat[:, block(j, 256)] = dot(act[...], proj_w[:, block(j, 256)]).astype(BF)

    loop(4, features)

    def joined(j):
        lin = dot(feat[...], in_w[:, block(j, 256)])
        sig = jax.nn.sigmoid(dot(feat[...], in_w[:, block(4 + j, 256)]))
        linear[:, block(j, 256)] = lin
        sigma[:, block(j, 256)] = sig
        glu[pl.ds(0, EXT), block(j, 256)] = (lin * sig).astype(BF).astype(F32)

    loop(4, joined)

    def mix(j):
        cols = block(j, 128)
        shift_all(shifts, glu, cols)
        for r in range(0, F, 64):
            total = jnp.zeros((64, 128), F32)
            for k in range(KW):
                rows = shifted(shifts, k, r, 64)
                total = total + taps[pl.ds(k, 1), cols] * (rows * linked[k, pl.ds(r, 64)])
            mixed[pl.ds(r, 64), cols] = total

    loop(8, mix)
    gain = depth_gain[...].astype(F32).reshape(1, D)

    def norm_all(i):
        rows = block(i, 32)
        v = mixed[rows, :]
        v = v - jnp.mean(v, axis=1, keepdims=True)
        scale = 1.0 / jnp.sqrt(jnp.mean(v * v, axis=1, keepdims=True) + EPS)
        v = v * scale
        inv[rows, :] = jnp.broadcast_to(scale, (32, 128))
        mixed[rows, :] = v
        scaled = v * gain
        s = jax.nn.sigmoid(scaled)
        dfac[rows, :] = s * (1.0 + scaled * (1.0 - s))
        dmix[pl.ds(pl.multiple_of(H + i * 32, 16), 32), :] = scaled * s

    loop(8, norm_all)

    def turn(j):
        cols = block(j, 256)
        swish_t[cols, :] = jnp.transpose(dmix[pl.ds(H, F), cols]).astype(BF)
        feat_t[cols, :] = jnp.transpose(feat[pl.ds(H, F), cols].astype(F32)).astype(BF)

    loop(4, turn)

    def turn_act(j):
        cols = block(j, 256)
        act_t[cols, :] = jnp.transpose(act[pl.ds(H, F), cols].astype(F32)).astype(BF)

    loop(2, turn_act)

    halos[2].wait_recv()
    r_f = lax.broadcasted_iota(jnp.int32, (F, 2 * F), 0)
    c_f = lax.broadcasted_iota(jnp.int32, (F, 2 * F), 1)
    r_h = lax.broadcasted_iota(jnp.int32, (F, 16), 0)
    c_h = lax.broadcasted_iota(jnp.int32, (F, 16), 1)
    first = (r_h == 0) & (c_h == 15) & (tm > 0)

    def one_hot(mask):
        return jnp.where(mask, 1.0, 0.0).astype(BF)

    for tap in range(3):
        rows = dot(one_hot(c_f == 2 * r_f + tap - 1), conv_in[...])
        if tap == 0:
            rows = rows + dot(one_hot(first), cin_halo[...])
        pairs[tap] = jnp.transpose(rows).astype(BF)

    loop(NTM - 1, lambda d: routed(d + 1).wait_recv())
    number = incoming[:, D : D + IDX].astype(F32)
    number = jnp.concatenate([number, number], axis=1)
    wanted = lax.broadcasted_iota(jnp.int32, (NTM * CAP, F), 1).astype(F32) + 1.0
    chosen = jnp.where(number == wanted, 1.0, 0.0)
    sel_t[...] = jnp.transpose(chosen).astype(BF)

    def place(j):
        up[pl.ds(0, F), block(j, 256)] = dot(sel_t[...], incoming[:, block(j, 256)]).astype(BF)

    loop(4, place)
    edge_up = remote(up.at[pl.ds(0, 16)], up.at[pl.ds(F, 16)], halo_send.at[3], halo_recv.at[3], left)
    edge_up.start()

    for one in loads[4:]:
        one.wait()

    def dswish(j):
        cols = block(j, 256)
        dfac[:, cols] = dfac[:, cols] * dot_nt(up[pl.ds(0, F), :], out_w[block(j, 256), :])

    loop(4, dswish)
    gainsum[...] = jnp.zeros((8, D), F32)

    def dnorm(i):
        rows = block(i, 32)
        ds = dfac[rows, :]
        v = mixed[rows, :]
        dv = ds * v
        gainsum[...] += dv[0:8] + dv[8:16] + dv[16:24] + dv[24:32]
        q = ds * gain
        q = q - jnp.mean(q, axis=1, keepdims=True) - v * jnp.mean(q * v, axis=1, keepdims=True)
        dmix[pl.ds(pl.multiple_of(H + i * 32, 16), 32), :] = inv[rows, pl.ds(0, 1)] * q

    loop(8, dnorm)
    edges = [
        remote(dmix.at[pl.ds(H, H)], dmix.at[pl.ds(H + F, H)], halo_send.at[4], halo_recv.at[4], left),
        remote(dmix.at[pl.ds(F, H)], dmix.at[pl.ds(0, H)], halo_send.at[5], halo_recv.at[5], right),
    ]
    for one in edges:
        one.start()

    def out_terms(half):
        def body(i):
            b = half * 2 + i
            cols = block(b, 256)
            term = dot(swish_t[...], up[pl.ds(0, F), cols]).astype(BF)
            for s in range(2):
                y = i * 2 + s
                p_out.g[half, y] = term[:, 128 * s : 128 * s + 128].reshape(NZ, NX, 32, 128)

        loop(2, body)

    out_terms(1 - at.c)
    p_out.start()
    out_terms(at.c)

    def depth(j):
        cols = block(j, 128)
        shift_all(shifts, glu, cols)
        total = [None] * KW
        for r in range(0, F, 64):
            grad = dmix[pl.ds(H + r, 64), cols]
            for k in range(KW):
                rows = shifted(shifts, k, r, 64)
                term = jnp.sum((rows * linked[k, pl.ds(r, 64)] * grad).reshape(8, 8, 128), axis=0)
                total[k] = term if r == 0 else total[k] + term
        for k in range(KW):
            dgs[k // 8, pl.ds(k % 8, 1), cols] = jnp.sum(total[k], axis=0, keepdims=True)

    p_out.over_core()

    for one in edges:
        one.wait_recv()
    edge_up.wait_recv()

    def dconv(j):
        cols = block(j, 128)
        gates = block(8 + j, 128)
        shift_all(shifts, dmix, cols)
        for r, size in ((0, 64), (64, 64), (128, 64), (192, 64), (256, 8)):
            total = jnp.zeros((size, 128), F32)
            for k in range(KW):
                rows = shifted(shifts, k, r, size)
                total = total + taps[pl.ds(KW - 1 - k, 1), cols] * (
                    rows * linked[k, pl.ds(r, size)]
                )
            sig = sigma[pl.ds(H + r, size), cols]
            ds = total * sig
            dg = ds * linear[pl.ds(H + r, size), cols] * (1.0 - sig)
            if size == 8:
                zero = jnp.zeros((8, 128), F32)
                ds = jnp.concatenate([ds, zero], axis=0)
                dg = jnp.concatenate([dg, zero], axis=0)
            dj[pl.ds(r, max(size, 16)), cols] = ds.astype(BF)
            dj[pl.ds(r, max(size, 16)), gates] = dg.astype(BF)

    loop(4, dconv)
    p_out.pass_on()
    loop(4, lambda j: dconv(4 + j))

    def in_terms(half):
        def body(y):
            term = dot(feat_t[...], dj[pl.ds(0, F), block(half * 4 + y, 256)]).astype(BF)
            for s in range(2):
                p_in.g[half, y, :, :, pl.ds(32 * s, 32), :] = term[
                    :, 128 * s : 128 * s + 128
                ].reshape(NZ, NX, 32, 128)

        loop(4, body)

    in_terms(1 - at.c)
    p_in.start()
    in_terms(at.c)
    p_out.over_first()

    def dfeatures(j):
        cols = block(j, 256)
        df[:, cols] = (up[:, cols].astype(F32) + dot_nt(dj[...], in_w[cols, :])).astype(BF)

    loop(4, dfeatures)
    p_in.over_core()

    def dpres(j):
        cols = block(j, 256)
        dpre[:, cols] = (dot_nt(df[...], proj_w[cols, :]) * slope[pl.ds(H, NEXT16), cols]).astype(BF)

    loop(2, dpres)

    def rest_terms(half):
        def body(i):
            cols = block(half * 2 + i, 256)
            term = dot(act_t[...], df[pl.ds(0, F), cols]).astype(BF)
            for s in range(2):
                y = i * 2 + s
                p_rest.g[half, y, :, :, pl.ds(0, 16), :] = term[
                    :, 128 * s : 128 * s + 128
                ].reshape(NZ, NX, 16, 128)

        loop(2, body)

    def conv_terms(tap, core, row):
        def body(i):
            term = dot(pairs[tap], dpre[pl.ds(0, F), block(i, 256)]).astype(BF)
            for s in range(2):
                p_rest.g[core, i * 2 + s, :, :, pl.ds(row, 16), :] = term[
                    :, 128 * s : 128 * s + 128
                ].reshape(NZ, NX, 16, 128)

        loop(2, body)

    rest_terms(0)
    rest_terms(1)
    for tap, core, row in ((0, 0, 16), (1, 0, 32), (2, 1, 16)):
        conv_terms(tap, core, row)
    p_rest.start()
    p_out.over_second()
    loop(2, depth)
    p_in.pass_on()
    p_rest.over_core()
    loop(3, lambda j: depth(2 + j))
    p_in.over_first()
    p_rest.pass_on()
    loop(3, lambda j: depth(5 + j))
    dgs[3, pl.ds(7, 1), :] = jnp.sum(gainsum[...], axis=0, keepdims=True)
    p_small.begin(dgs)
    factor = 1.0 / math.sqrt(F * NTM * 8)
    p_out.over_z(factor)

    r_o = lax.broadcasted_iota(jnp.int32, (2 * F, NEXT16), 0)
    c_o = lax.broadcasted_iota(jnp.int32, (2 * F, NEXT16), 1)
    here = dot(one_hot(r_o == 2 * c_o), dpre[...]).astype(BF)
    here_odd = dot(one_hot(r_o == 2 * c_o + 1), dpre[...]).astype(BF)
    ahead = (r_o == 2 * c_o - 1) & ((c_o < F) | (tm < NTM - 1))
    ahead = dot(one_hot(ahead), dpre[...]).astype(BF)
    o_input[...] = dot_nt(here, conv_w[1])
    o_input[...] += dot_nt(here_odd, conv_w[2])
    o_input[...] += dot_nt(ahead, conv_w[0])

    p_small.second()
    p_in.over_second()
    p_rest.over_first()
    p_small.third()
    p_in.over_z(factor)
    p_rest.over_second(p_small.join)
    p_out.gathered()
    o_fin_out[...] = p_out.fin[...]
    p_in.gathered()
    o_fin_in[...] = p_in.fin[...]
    p_rest.over_z(factor)
    p_rest.gathered()
    o_fin_rest[...] = p_rest.fin[...]

    loop(NTM - 1, lambda d: routed(d + 1).wait_send())
    for one in halos + [edge_up] + edges:
        one.wait_send()
    for part in (p_out, p_in, p_rest, p_small):
        part.close()


def spread(
    rows, f_out, f_in, f_rest, o_input, o_conv, o_proj, o_in, o_depth, o_gain, o_out, done
):
    whole = pltpu.make_async_copy(rows, o_input, done)
    whole.start()
    for b in range(8):
        cols = pl.ds(128 * b, 128)
        o_out[:, cols] = f_out[b].astype(F32)
        o_proj[:, cols] = f_rest[b, pl.ds(0, 16)].astype(F32)
        for s in range(2):
            o_in[:, pl.ds(256 * b + 128 * s, 128)] = f_in[b, pl.ds(32 * s, 32)].astype(F32)
    x = lax.rem(lax.axis_index("tm"), NX)
    for y in range(NY):
        cols = pl.ds(128 * y, 128)
        o_conv[0, :, cols] = f_rest[y, pl.ds(16, 16)].astype(F32)
        o_conv[1, :, cols] = f_rest[y, pl.ds(32, 16)].astype(F32)
        o_conv[2, :, cols] = f_rest[NY + y, pl.ds(16, 16)].astype(F32)
        small = f_rest[NY + y, pl.ds(32, 16)].astype(F32)[0:8]
        mine = jnp.zeros((8, 32), F32)
        for other in range(NX):
            mine = mine + jnp.where(x == other, small[:, 32 * other : 32 * other + 32], 0.0)
        if y < NY - 1:
            o_depth[pl.ds(8 * y, 8), :] = mine
        else:
            o_depth[pl.ds(8 * y, 7), :] = mine[0:7]
            o_gain[...] = mine[7:8]
    whole.wait()


def per_device(
    grad_attn, route, lengths, conv_pre, conv_in, conv_w, proj_w, in_w, depth_w, depth_gain, out_w
):
    vmem = pl.BlockSpec(memory_space=pltpu.VMEM)
    anywhere = pl.BlockSpec(memory_space=pl.ANY)
    smem = pl.BlockSpec(memory_space=pltpu.SMEM)
    scratch = [
        pltpu.VMEM((NTM * CAP, D + IDX), BF),
        pltpu.VMEM((NTM * CAP, D + IDX), BF),
        pltpu.VMEM((EXT, CF), BF),
        pltpu.VMEM((16, CF), BF),
        pltpu.VMEM((KW, NEXT, 128), F32),
        pltpu.VMEM((PAD, 128), jnp.int32),
        pltpu.VMEM((EXT, CF), BF),
        pltpu.VMEM((EXT, CF), F32),
        pltpu.VMEM((EXT, D), BF),
        pltpu.VMEM((EXT, D), F32),
        pltpu.VMEM((EXT, D), F32),
        pltpu.VMEM((PAD, D), F32),
        pltpu.VMEM((F, D), F32),
        pltpu.VMEM((D, F), BF),
        pltpu.VMEM((F, D), F32),
        pltpu.VMEM((F, 128), F32),
        pltpu.VMEM((PAD, D), F32),
        pltpu.VMEM((NEXT16, D), BF),
        pltpu.VMEM((NTM * CAP, F), BF),
        pltpu.VMEM((32, D), F32),
        pltpu.VMEM((8, D), F32),
        pltpu.VMEM((NEXT16, 2 * D), BF),
        pltpu.VMEM((NEXT16, D), BF),
        pltpu.VMEM((NEXT16, CF), BF),
        pltpu.VMEM((D, F), BF),
        pltpu.VMEM((CF, F), BF),
        pltpu.VMEM((F, NTM * CAP), BF),
        pltpu.VMEM((3, CF, F), BF),
        pltpu.VMEM((4, 16, D), F32),
        pltpu.VMEM((8, EXT, 128), F32),
        pltpu.VMEM((2 * F, CF), BF),
        pltpu.VMEM((3, CF, CF), BF),
        pltpu.VMEM((CF, D), BF),
        pltpu.VMEM((D, 2 * D), BF),
        pltpu.VMEM((D, D), BF),
        pltpu.SemaphoreType.DMA((6,)),
        pltpu.SemaphoreType.DMA((NTM,)),
        pltpu.SemaphoreType.DMA((NTM,)),
        pltpu.SemaphoreType.DMA((6,)),
        pltpu.SemaphoreType.DMA((6,)),
    ]
    for rows in PART_ROWS:
        scratch += part_scratch(rows)
    scratch += [
        pltpu.VMEM((NY, 16, D), BF),
        pltpu.VMEM((NY, 16, D), BF),
        pltpu.VMEM((3, 16, D), BF),
        pltpu.VMEM((16, D), BF),
        pltpu.VMEM((3, 16, D), BF),
        pltpu.SemaphoreType.DMA((7,)),
        pltpu.SemaphoreType.DMA((7,)),
    ]
    outs = pl.pallas_call(
        kernel,
        out_shape=[jax.ShapeDtypeStruct((2 * F, CF), F32)]
        + [jax.ShapeDtypeStruct((8, rows, 128), BF) for rows in PART_ROWS],
        in_specs=[smem] + [vmem] * 2 + [anywhere] * 5 + [vmem] * 2 + [anywhere],
        out_specs=[vmem] * 4,
        scratch_shapes=scratch,
        compiler_params=pltpu.CompilerParams(
            collective_id=0, has_side_effects=True, vmem_limit_bytes=62 * 2**20
        ),
    )(
        lengths, route, grad_attn[0], conv_pre[0], conv_in[0], conv_w, proj_w, in_w, depth_w,
        depth_gain, out_w,
    )
    o_input, o_conv, o_proj, o_in, o_depth, o_gain, o_out = pl.pallas_call(
        spread,
        out_shape=[
            jax.ShapeDtypeStruct((2 * F, CF), F32),
            jax.ShapeDtypeStruct((3, 16, CF), F32),
            jax.ShapeDtypeStruct((16, D), F32),
            jax.ShapeDtypeStruct((32, 2 * D), F32),
            jax.ShapeDtypeStruct((KW, 32), F32),
            jax.ShapeDtypeStruct((1, 32), F32),
            jax.ShapeDtypeStruct((32, D), F32),
        ],
        in_specs=[vmem] * 4,
        out_specs=[anywhere] + [vmem] * 6,
        scratch_shapes=[pltpu.SemaphoreType.DMA],
    )(*outs)
    return (o_input[None], o_conv, o_proj, o_in, o_depth, o_gain[0], o_out)


def solution(mesh):
    placed = (
        P("dp", "tm", None),
        P("dp", "tm"),
        P("dp", None),
        P("dp", "tm", None),
        P("dp", "tm", None),
        P(),
        P(),
        P(),
        P(),
        P(),
        P(),
    )
    return jax.shard_map(
        per_device,
        mesh=mesh,
        in_specs=placed,
        out_specs=(
            P("dp", "tm", None),
            P(None, "tm", None),
            P("tm", None),
            P("tm", None),
            P(None, "tm"),
            P("tm"),
            P("tm", None),
        ),
        check_vma=False,
    )
```
